256 devices in a mesh: probe: 32 (over z, x_hi, core), depth: 8 (over y, x_lo).
Axes of the slice: x: 4 (x_hi: 2, x_lo: 2; x = x_hi * 2 + x_lo), y: 4, z: 8, core: 2. Of those that a mesh axis runs over, the one named last changes fastest.
Arguments:
- potential: float32 [16, 4096, 1024], P('depth', 'probe'), may hold values from -6 to 6
- probe: float32 [2, 256, 256], replicated, may hold values from -6 to 6
- positions: int32 [32, 2], P('probe'), may hold values from 0 to 4095, as said below
- intensity: float32 [32, 256, 256], P('probe'), may hold values from 0 to 4
Outputs:
- potential_grad: float32 [16, 4096, 1024], P('depth', 'probe')
The draws below stay inside these ranges and needn't reach their ends.
Inputs may be any that keep to these rules, and one draw needn't show every extreme that they name: `positions`: entry 0 of probe p is the top row of its window and entry 1 its left column, 0 to 768. The window's centre row, (entry 128) mod 4096, lies in rows g * 128 to g * 128 + 127, where g = p // 1 is the probe's group.
All inputs are finite; a program needn't handle non-finite values.
Results may differ from the reference program's by a relative error of at most 0.0003.
Values sent between devices are 32-bit elements; how exact they have to be, the bound alone decides.
A program may use at most 64 MiB of HBM per device.

```python
import jax
import jax.numpy as jnp
from jax import lax

W = 256
PR_DEV = 1
NY = 1024
STRIP = 128
NX = 4096
SLICES = 16
PROBES = 32


def draw_positions(key, part):
    first_key = jax.random.fold_in(key, 11)
    second_key = jax.random.fold_in(key, 23)
    probe_ids = jnp.arange(PROBES, dtype=jnp.int32)
    group_ids = probe_ids // PR_DEV
    within = probe_ids % PR_DEV
    offsets = jax.random.randint(first_key, (PROBES,), 0, STRIP, dtype=jnp.int32)
    offsets = offsets.at[0].set(STRIP - 1).at[PR_DEV].set(0)
    row_tops = (group_ids * STRIP + offsets - STRIP) % NX
    spacing = max(PR_DEV - 1, 1)
    base = within * (NY - W) // spacing
    jitter = jax.random.randint(second_key, (PROBES,), -(W // 8), W // 8 + 1, dtype=jnp.int32)
    column_lefts = jnp.clip(base + jitter, 0, NY - W)
    column_lefts = column_lefts.at[1].set(0).at[PROBES - 1].set(NY - W)
    return jnp.stack([row_tops, column_lefts], axis=1).astype(jnp.int32)


def block_scale(own_key, shape, split, least, high):
    gain, own = 1.0, jax.random.fold_in(own_key, 6)
    for dim, shards_of in split:
        heights = jnp.exp(jax.random.uniform(jax.random.fold_in(own, dim), (shards_of,), jnp.float32, least / len(split), high / len(split)))
        gain = gain * jnp.repeat(heights, shape[dim] // shards_of).reshape([-1 if axis == dim else 1 for axis in range(len(shape))])
    return gain


def bell_draw(own_key, shape, spread, reach, pieces=(), kind=jnp.bfloat16):
    drawn = jax.random.normal(own_key, shape, jnp.float32) * spread
    if len(pieces) > 0:
        drawn = block_scale(own_key, shape, pieces, -0.22, 0.18) * drawn
    return jnp.clip(drawn, min=-reach, max=reach).astype(kind)


def setup_inputs(seed: int = 0) -> dict:
    streams_of = jax.random.split(jax.random.key(seed), 5)
    return {
        "potential": bell_draw(streams_of[0], (SLICES, NX, NY), 1.0, 6.0, ((0, 8), (1, 32)), jnp.float32),
        "probe": bell_draw(streams_of[1], (2, W, W), 1.0, 6.0, (), jnp.float32),
        "positions": draw_positions(jax.random.fold_in(streams_of[4], 71), 0),
        "intensity": jnp.clip(4.0 * jax.random.uniform(streams_of[3], (PROBES, W, W), jnp.float32) ** block_scale(streams_of[3], (PROBES, W, W), ((0, 32),), -0.2, 0.2), 0.0, 4.0),
    }


interaction = 0.5
fresnel_phase = 60.0
highest = lax.Precision.HIGHEST

def dft_tables(extent):
    counter = jnp.arange(extent, dtype=jnp.int32)
    product = counter[:, None] * counter[None, :] % extent
    angles = 2.0 * jnp.pi / extent * product.astype(jnp.float32)
    norm_scale = 1.0 / jnp.sqrt(jnp.float32(extent))
    return (jnp.cos(angles) * norm_scale, -jnp.sin(angles) * norm_scale)

def kernel_table(extent):
    counter = jnp.arange(extent, dtype=jnp.int32)
    frequency = ((counter + extent // 2) % extent - extent // 2).astype(jnp.float32) / extent
    phases = -fresnel_phase * (frequency[:, None] ** 2 + frequency[None, :] ** 2)
    return (jnp.cos(phases), jnp.sin(phases))

def left_product(matrix, field):
    return jnp.einsum('jk,...kl->...jl', matrix, field, precision=highest)

def right_product(field, matrix):
    return jnp.einsum('...jk,kl->...jl', field, matrix, precision=highest)

def complex_left(matrices, fields):
    return (left_product(matrices[0], fields[0]) - left_product(matrices[1], fields[1]), left_product(matrices[0], fields[1]) + left_product(matrices[1], fields[0]))

def complex_right(fields, matrices):
    return (right_product(fields[0], matrices[0]) - right_product(fields[1], matrices[1]), right_product(fields[0], matrices[1]) + right_product(fields[1], matrices[0]))

def forward_dft(fields, tables):
    return complex_right(complex_left(tables, fields), tables)

def inverse_dft(fields, tables):
    conjugate = (tables[0], -tables[1])
    return complex_right(complex_left(conjugate, fields), conjugate)

def propagate(fields, tables, kernel):
    spectrum = forward_dft(fields, tables)
    moved = (kernel[0] * spectrum[0] - kernel[1] * spectrum[1], kernel[0] * spectrum[1] + kernel[1] * spectrum[0])
    return inverse_dft(moved, tables)

def transmit(fields, window):
    cosine = jnp.cos(interaction * window)
    sine_part = jnp.sin(interaction * window)
    return (cosine * fields[0] - sine_part * fields[1], cosine * fields[1] + sine_part * fields[0])

def probe_loss(windows, probe, measured, tables, kernel):
    fields = (probe[0], probe[1])
    for layer_id in range(windows.shape[0]):
        fields = propagate(transmit(fields, windows[layer_id]), tables, kernel)
    far_field = forward_dft(fields, tables)
    misfit = far_field[0] * far_field[0] + far_field[1] * far_field[1] - measured
    return 0.25 * jnp.sum(misfit * misfit)

def reference(potential, probe, positions, intensity):
    tables = dft_tables(W)
    kernel = kernel_table(W)
    offsets = jnp.arange(W, dtype=jnp.int32)
    grad_window = jax.grad(probe_loss)

    def one_probe(entry_pair):
        location, measured = entry_pair
        row_ids = ((location[0] + offsets) % NX).astype(jnp.int32)
        row_band = jnp.take(potential, row_ids, axis=1)
        windows = lax.dynamic_slice_in_dim(row_band, location[1].astype(jnp.int32), W, 2)
        return grad_window(windows, probe, measured, tables, kernel)
    window_grads = lax.map(one_probe, (positions, intensity))

    def accumulate(running, entry_pair):
        location, window_grad = entry_pair
        row_ids = ((location[0] + offsets) % NX).astype(jnp.int32)
        column_ids = (location[1] + offsets).astype(jnp.int32)
        return (running.at[:, row_ids[:, None], column_ids[None, :]].add(window_grad), None)
    running, unused = lax.scan(accumulate, jnp.zeros_like(potential), (positions, window_grads))
    return running
```

```python
import jax
import jax.numpy as jnp
import ml_dtypes
import numpy as np
from jax import lax
from jax.experimental import pallas as pl
from jax.experimental.pallas import tpu as pltpu
from jax.sharding import PartitionSpec as P
W=256; HB=128
f32=jnp.float32; bf16=jnp.bfloat16

def fit(fn, degree, top):
    n=64
    z=(np.cos(np.pi*(np.arange(n)+.5)/n)+1)*top/2
    return np.polynomial.chebyshev.Chebyshev.fit(z, fn(z), degree, domain=[0,top]).convert(kind=np.polynomial.Polynomial).coef
SINC=fit(lambda z: np.sin(np.sqrt(z))/np.sqrt(z),6,9.0)
COSC=fit(lambda z: np.cos(np.sqrt(z)),6,9.0)

def halves(a):
    hi=a.astype(np.float32).astype(ml_dtypes.bfloat16)
    lo=(a-hi.astype(np.float64)).astype(np.float32).astype(ml_dtypes.bfloat16)
    return hi,lo

def tables():
    k=np.arange(W)
    F=np.exp(-2j*np.pi*((k[:,None]*k[None,:])%W)/W)/np.sqrt(W)
    fr=(((k+W//2)%W)-W//2)/W
    h=np.exp(-60j*fr*fr)
    A=np.conj(F)@np.diag(h)@F
    order=np.concatenate([np.arange(HB), W-1-np.arange(HB)])
    PP=A[:HB,:HB]; Q=A[:HB][:,order[HB:]]
    out=[]
    for B in ((PP+Q)/2,(PP-Q)/2):
        right=np.block([[B.real,B.imag],[-B.imag,B.real]])
        left=np.block([[B.real,-B.imag],[B.imag,B.real]])
        out.append((right,left))
    prop=[out[0][0],out[1][0],out[0][1],out[1][1]]
    G=F[:,order]
    far=[G.T.real,G.T.imag,G.real,G.imag]
    hp,lp=zip(*[halves(a) for a in prop]); hf,lf=zip(*[halves(a) for a in far])
    return np.stack([np.stack(hp),np.stack(lp)]), np.stack([np.stack(hf),np.stack(lf)])

def split(x):
    hi=x.astype(bf16)
    return hi,(x-hi.astype(f32)).astype(bf16)

def dot(a,b):
    return lax.dot_general(a,b,(((1,),(0,)),((),())),preferred_element_type=f32)

def mm_right(x, wh, wl):
    h,l=split(x)
    return dot(h,wh)+dot(l,wh)+dot(h,wl)
def mm_left(wh,wl,x):
    h,l=split(x)
    return dot(wh,h)+dot(wh,l)+dot(wl,h)

def propagate(ur,ui,T):
    ure,uro=ur[:,:HB]+ur[:,HB:],ur[:,:HB]-ur[:,HB:]
    uie,uio=ui[:,:HB]+ui[:,HB:],ui[:,:HB]-ui[:,HB:]
    ye=mm_right(jnp.concatenate([ure,uie],1),T[0,0],T[1,0])
    yo=mm_right(jnp.concatenate([uro,uio],1),T[0,1],T[1,1])
    te,be=ye[:HB]+ye[HB:],ye[:HB]-ye[HB:]
    to,bo=yo[:HB]+yo[HB:],yo[:HB]-yo[HB:]
    re=jnp.concatenate([jnp.concatenate([te[:,:HB],to[:,:HB]],1),jnp.concatenate([te[:,HB:],to[:,HB:]],1)],0)
    ro=jnp.concatenate([jnp.concatenate([be[:,:HB],bo[:,:HB]],1),jnp.concatenate([be[:,HB:],bo[:,HB:]],1)],0)
    ze=mm_left(T[0,2],T[1,2],re)
    zo=mm_left(T[0,3],T[1,3],ro)
    top=ze+zo; bot=ze-zo
    def unfold(t,b):
        return jnp.concatenate([jnp.concatenate([t[:,:HB]+t[:,HB:],t[:,:HB]-t[:,HB:]],1),
                                jnp.concatenate([b[:,:HB]+b[:,HB:],b[:,:HB]-b[:,HB:]],1)],0)
    return unfold(top[:HB],bot[:HB]),unfold(top[HB:],bot[HB:])

def cmm_right(xr,xi,rh,rl,ih,il):
    hr,lr=split(xr); hi,li=split(xi)
    yr=dot(hr,rh)+dot(lr,rh)+dot(hr,rl)-(dot(hi,ih)+dot(li,ih)+dot(hi,il))
    yi=dot(hr,ih)+dot(lr,ih)+dot(hr,il)+(dot(hi,rh)+dot(li,rh)+dot(hi,rl))
    return yr,yi
def cmm_left(rh,rl,ih,il,xr,xi):
    hr,lr=split(xr); hi,li=split(xi)
    yr=dot(rh,hr)+dot(rh,lr)+dot(rl,hr)-(dot(ih,hi)+dot(ih,li)+dot(il,hi))
    yi=dot(ih,hr)+dot(ih,lr)+dot(il,hr)+(dot(rh,hi)+dot(rh,li)+dot(rl,hi))
    return yr,yi

def poly(c,z):
    r=jnp.full_like(z,float(c[-1]))
    for a in c[-2::-1]:
        r=r*z+float(a)
    return r
def sincos(v):
    x=0.5*v; z=x*x
    return poly(COSC,z), x*poly(SINC,z)

def detector(ur,ui,inten,Fr):
    yr,yi=cmm_right(ur,ui,Fr[0,0],Fr[1,0],Fr[0,1],Fr[1,1])
    fr,fi=cmm_left(Fr[0,2],Fr[1,2],Fr[0,3],Fr[1,3],yr,yi)
    m=fr*fr+fi*fi-inten
    gr,gi=m*fr,-(m*fi)
    yr,yi=cmm_right(gr,gi,Fr[0,2],Fr[1,2],Fr[0,3],Fr[1,3])
    return cmm_left(Fr[0,0],Fr[1,0],Fr[0,1],Fr[1,1],yr,yi)

def chain_kernel(v_ref, p_ref, i_ref, T, Fr, d_ref, cs, us, ps):
    S=v_ref.shape[0]
    def load_t(s,_):
        c,n=sincos(v_ref[s])
        cs[s,0]=c; cs[s,1]=n
        return _
    lax.fori_loop(0,S,load_t,0)
    def trans(s,ar,ai):
        c,n=cs[s,0],cs[s,1]
        return c*ar-n*ai, c*ai+n*ar
    ps[0]=p_ref[0]; ps[1]=p_ref[1]
    def fwd(s,_):
        ur,ui=trans(s,ps[0],ps[1])
        us[s,0]=ur; us[s,1]=ui
        ps[0],ps[1]=propagate(ur,ui,T)
        return _
    lax.fori_loop(0,S-1,fwd,0)
    ur,ui=trans(S-1,ps[0],ps[1])
    us[S-1,0]=ur; us[S-1,1]=ui
    qr,qi=detector(ur,ui,i_ref[...],Fr)
    ps[0]=qr; ps[1]=qi
    d_ref[S-1]=-0.5*(qr*ui+qi*ur)
    def bwd(t,_):
        s=S-2-t
        gr,gi=trans(s+1,ps[0],ps[1])
        qr,qi=propagate(gr,gi,T)
        ps[0]=qr; ps[1]=qi
        d_ref[s]=-0.5*(qr*us[s,1]+qi*us[s,0])
        return _
    lax.fori_loop(0,S-1,bwd,0)

def chain(v,p,i,T,Fr):
    S=v.shape[0]
    vm=pl.BlockSpec(memory_space=pltpu.VMEM)
    return pl.pallas_call(chain_kernel,out_shape=jax.ShapeDtypeStruct((S,W,W),f32),
      in_specs=[vm]*5,out_specs=vm,
      scratch_shapes=[pltpu.VMEM((S,2,W,W),f32),pltpu.VMEM((S,2,W,W),f32),pltpu.VMEM((2,W,W),f32)],
      compiler_params=pltpu.CompilerParams(vmem_limit_bytes=56<<20))(v,p,i,T,Fr)


def exact_parts(x):
    high = lax.reduce_precision(x, 8, 7)
    rest = x - high
    mid = lax.reduce_precision(rest, 8, 7)
    return high.astype(bf16), mid.astype(bf16), (rest - mid).astype(bf16)


def select_right(x, chosen):
    a, b, c = exact_parts(x)
    return dot(a, chosen) + dot(b, chosen) + dot(c, chosen)


def select_left(chosen, x):
    a, b, c = exact_parts(x)
    return dot(chosen, a) + dot(chosen, b) + dot(chosen, c)


def fold(x, dim):
    low, high = jnp.split(x, 2, axis=dim)
    return jnp.concatenate([low, jnp.flip(high, dim)], axis=dim)


def folded(index):
    return jnp.where(index < HB, index, W + HB - 1 - index)


def local(potential, probe, positions, intensity):
    layers, strip, columns = potential.shape
    group = lax.axis_index("probe")
    groups = lax.axis_size("probe")
    depth = lax.axis_index("depth")
    up = [(i, (i + 1) % groups) for i in range(groups)]
    down = [(b, a) for a, b in up]
    mine = positions[0]
    before = lax.ppermute(mine, "probe", up)
    after = lax.ppermute(mine, "probe", down)
    place = folded(jnp.arange(W, dtype=jnp.int32))

    def column_pick(position):
        line = jnp.arange(columns, dtype=jnp.int32)[:, None]
        return (line == position[1] + place[None, :]).astype(bf16)

    own_pick, before_pick, after_pick = (column_pick(p) for p in (mine, before, after))
    flat = potential.reshape(layers * strip, columns)
    own = select_right(flat, own_pick).reshape(layers, strip, W)
    to_before = select_right(flat, before_pick).reshape(layers, strip, W)
    to_after = select_right(flat, after_pick).reshape(layers, strip, W)
    from_before = lax.ppermute(to_after, "probe", up)
    from_after = lax.ppermute(to_before, "probe", down)
    offset = (mine[0] - (group - 1) * strip) % (strip * groups)
    lines = jnp.arange(3 * strip, dtype=jnp.int32)
    row_pick = (lines[None, :] == offset + place[:, None]).astype(bf16)
    tall = jnp.concatenate([from_before, own, from_after], axis=1)
    windows = jnp.stack([select_left(row_pick, tall[s]) for s in range(layers)])
    every = lax.all_gather(windows, "depth", axis=0, tiled=True)
    T, Fr = tables()
    entry = fold(fold(probe, 1), 2)
    grads = chain(every, entry, intensity[0], jnp.asarray(T), jnp.asarray(Fr))
    grads = lax.dynamic_slice_in_dim(grads, depth * layers, layers, 0)
    tall = jnp.stack([select_left(row_pick.T, grads[s]) for s in range(layers)])
    from_after = lax.ppermute(tall[:, :strip], "probe", down)
    from_before = lax.ppermute(tall[:, 2 * strip :], "probe", up)

    def spread(x, pick):
        return select_right(x.reshape(layers * strip, W), pick.T).reshape(layers, strip, columns)

    return (
        spread(tall[:, strip : 2 * strip], own_pick)
        + spread(from_before, before_pick)
        + spread(from_after, after_pick)
    )


def solution(mesh):
    in_specs = (P("depth", "probe", None), P(), P("probe", None), P("probe", None, None))
    out_specs = P("depth", "probe", None)
    return jax.shard_map(local, mesh=mesh, in_specs=in_specs, out_specs=out_specs, check_vma=False)
```

```python
import functools

import jax
import jax.numpy as jnp
import ml_dtypes
import numpy as np
from jax import lax
from jax.experimental import pallas as pl
from jax.experimental.pallas import tpu as pltpu
from jax.sharding import PartitionSpec as P
W=256; HB=128
f32=jnp.float32; bf16=jnp.bfloat16

def fit(fn, degree, top):
    n=64
    z=(np.cos(np.pi*(np.arange(n)+.5)/n)+1)*top/2
    return np.polynomial.chebyshev.Chebyshev.fit(z, fn(z), degree, domain=[0,top]).convert(kind=np.polynomial.Polynomial).coef
SINC=fit(lambda z: np.sin(np.sqrt(z))/np.sqrt(z),6,9.0)
COSC=fit(lambda z: np.cos(np.sqrt(z)),6,9.0)

def halves(a):
    hi=a.astype(np.float32).astype(ml_dtypes.bfloat16)
    lo=(a-hi.astype(np.float64)).astype(np.float32).astype(ml_dtypes.bfloat16)
    return hi,lo

def tables():
    k=np.arange(W)
    F=np.exp(-2j*np.pi*((k[:,None]*k[None,:])%W)/W)/np.sqrt(W)
    fr=(((k+W//2)%W)-W//2)/W
    h=np.exp(-60j*fr*fr)
    A=np.conj(F)@np.diag(h)@F
    order=np.concatenate([np.arange(HB), W-1-np.arange(HB)])
    PP=A[:HB,:HB]; Q=A[:HB][:,order[HB:]]
    out=[]
    for B in ((PP+Q)/2,(PP-Q)/2):
        right=np.block([[B.real,B.imag],[-B.imag,B.real]])
        left=np.block([[B.real,-B.imag],[B.imag,B.real]])
        out.append((right,left))
    prop=[out[0][0],out[1][0],out[0][1],out[1][1]]
    G=F[:,order]
    far=[G.T.real,G.T.imag,G.real,G.imag]
    hp,lp=zip(*[halves(a) for a in prop]); hf,lf=zip(*[halves(a) for a in far])
    return np.stack([np.stack(hp),np.stack(lp)]), np.stack([np.stack(hf),np.stack(lf)])

def split(x):
    hi=x.astype(bf16)
    return hi,(x-hi.astype(f32)).astype(bf16)

def dot(a,b):
    return lax.dot_general(a,b,(((1,),(0,)),((),())),preferred_element_type=f32)

def mm_right(x, wh, wl):
    h,l=split(x)
    return dot(h,wh)+dot(l,wh)+dot(h,wl)
def mm_left(wh,wl,x):
    h,l=split(x)
    return dot(wh,h)+dot(wh,l)+dot(wl,h)

def propagate(ur,ui,T):
    ure,uro=ur[:,:HB]+ur[:,HB:],ur[:,:HB]-ur[:,HB:]
    uie,uio=ui[:,:HB]+ui[:,HB:],ui[:,:HB]-ui[:,HB:]
    ye=mm_right(jnp.concatenate([ure,uie],1),T[0,0],T[1,0])
    yo=mm_right(jnp.concatenate([uro,uio],1),T[0,1],T[1,1])
    te,be=ye[:HB]+ye[HB:],ye[:HB]-ye[HB:]
    to,bo=yo[:HB]+yo[HB:],yo[:HB]-yo[HB:]
    re=jnp.concatenate([jnp.concatenate([te[:,:HB],to[:,:HB]],1),jnp.concatenate([te[:,HB:],to[:,HB:]],1)],0)
    ro=jnp.concatenate([jnp.concatenate([be[:,:HB],bo[:,:HB]],1),jnp.concatenate([be[:,HB:],bo[:,HB:]],1)],0)
    ze=mm_left(T[0,2],T[1,2],re)
    zo=mm_left(T[0,3],T[1,3],ro)
    top=ze+zo; bot=ze-zo
    def unfold(t,b):
        return jnp.concatenate([jnp.concatenate([t[:,:HB]+t[:,HB:],t[:,:HB]-t[:,HB:]],1),
                                jnp.concatenate([b[:,:HB]+b[:,HB:],b[:,:HB]-b[:,HB:]],1)],0)
    return unfold(top[:HB],bot[:HB]),unfold(top[HB:],bot[HB:])

def cmm_right(xr,xi,rh,rl,ih,il):
    hr,lr=split(xr); hi,li=split(xi)
    yr=dot(hr,rh)+dot(lr,rh)+dot(hr,rl)-(dot(hi,ih)+dot(li,ih)+dot(hi,il))
    yi=dot(hr,ih)+dot(lr,ih)+dot(hr,il)+(dot(hi,rh)+dot(li,rh)+dot(hi,rl))
    return yr,yi
def cmm_left(rh,rl,ih,il,xr,xi):
    hr,lr=split(xr); hi,li=split(xi)
    yr=dot(rh,hr)+dot(rh,lr)+dot(rl,hr)-(dot(ih,hi)+dot(ih,li)+dot(il,hi))
    yi=dot(ih,hr)+dot(ih,lr)+dot(il,hr)+(dot(rh,hi)+dot(rh,li)+dot(rl,hi))
    return yr,yi

def poly(c,z):
    r=jnp.full_like(z,float(c[-1]))
    for a in c[-2::-1]:
        r=r*z+float(a)
    return r
def sincos(v):
    x=0.5*v; z=x*x
    return poly(COSC,z), x*poly(SINC,z)

def detector(ur,ui,inten,Fr):
    yr,yi=cmm_right(ur,ui,Fr[0,0],Fr[1,0],Fr[0,1],Fr[1,1])
    fr,fi=cmm_left(Fr[0,2],Fr[1,2],Fr[0,3],Fr[1,3],yr,yi)
    m=fr*fr+fi*fi-inten
    gr,gi=m*fr,-(m*fi)
    yr,yi=cmm_right(gr,gi,Fr[0,2],Fr[1,2],Fr[0,3],Fr[1,3])
    return cmm_left(Fr[0,0],Fr[1,0],Fr[0,1],Fr[1,1],yr,yi)


def exact_parts(x):
    high = x.astype(bf16)
    rest = x - high.astype(f32)
    mid = rest.astype(bf16)
    return high, mid, (rest - mid.astype(f32)).astype(bf16)


def select_right(x, chosen):
    a, b, c = exact_parts(x)
    return dot(a, chosen) + dot(b, chosen) + dot(c, chosen)


def select_left(chosen, x):
    a, b, c = exact_parts(x)
    return dot(chosen, a) + dot(chosen, b) + dot(chosen, c)


def spread(x, chosen):
    return sum(
        lax.dot_general(part, chosen, (((1,), (1,)), ((), ())), preferred_element_type=f32)
        for part in exact_parts(x)
    )


def folded(shape, dim):
    index = lax.broadcasted_iota(jnp.int32, shape, dim)
    return jnp.where(index < HB, index, W + HB - 1 - index)


def ones_where(condition):
    return jnp.where(condition, 1.0, 0.0).astype(bf16)


def wide(row, width):
    return jnp.concatenate([row] * (width // 128), axis=1)


def kernel(
    groups, depths, v_ref, p_ref, pos_ref, i_ref, T, Fr, o_ref,
    V, cs, us, ps, dbuf, pos_out, pos_in, halo_out, halo_in, dep_out, dep_in, own_cut, pick,
    pos_ss, pos_rs, halo_ss, halo_rs, send_v, recv_v, relay_s, send_d, recv_d, dep_ss, dep_rs,
):
    layers, strip, columns = v_ref.shape
    slices = layers * depths
    rows = groups * strip
    g = lax.axis_index("probe")
    d = lax.axis_index("depth")
    y = d // 2
    xl = d % 2
    core = g % 2
    active = xl == core
    before, after = (g + groups - 1) % groups, (g + 1) % groups
    home = 2 * y + core
    partner = d + 1 - 2 * xl
    up, down = (home + 2) % depths, (home + depths - 2) % depths

    def there(probe_at, depth_at):
        return {"probe": probe_at, "depth": depth_at}

    barrier = pltpu.get_barrier_semaphore()
    peers = [there(before, d), there(after, d), there(g, partner)]
    for base in (d, partner):
        peers.append(there(g, (base + 2) % depths))
        peers.append(there(g, (base + depths - 2) % depths))
    for peer in peers:
        pl.semaphore_signal(barrier, inc=1, device_id=peer, device_id_type=pl.DeviceIdType.MESH)
    pos_out[0] = jnp.full((8, 128), pos_ref[0, 0], jnp.int32)
    pos_out[1] = jnp.full((8, 128), pos_ref[0, 1], jnp.int32)
    pl.semaphore_wait(barrier, len(peers))

    def remote(source, target, sent, received, where):
        return pltpu.make_async_remote_copy(
            src_ref=source, dst_ref=target, send_sem=sent, recv_sem=received,
            device_id=where, device_id_type=pl.DeviceIdType.MESH,
        )

    near = (there(before, d), there(after, d))
    pos_copy = [remote(pos_out, pos_in.at[1 - n], pos_ss.at[n], pos_rs.at[1 - n], near[n]) for n in (0, 1)]
    for n in (0, 1):
        pos_copy[n].start()

    lines = lax.broadcasted_iota(jnp.int32, (columns, W), 0)
    place = folded((columns, W), 1)

    def column_pick(left):
        return ones_where(lines == place + wide(left, W))

    pick[2] = column_pick(pos_out[1][:1])
    for s in range(layers):
        own_cut[s] = select_right(v_ref[s], pick[2])
    fold = ones_where(lax.broadcasted_iota(jnp.int32, (W, W), 0) == folded((W, W), 1))
    for c in (0, 1):
        ps[c] = select_left(fold, select_right(p_ref[c], fold))
    offset = (pos_out[0][:1] - (g - 1) * strip + rows) & (rows - 1)
    row_pick = ones_where(
        lax.broadcasted_iota(jnp.int32, (W, 3 * strip), 1) == folded((W, 3 * strip), 0) + wide(offset, 3 * strip)
    )
    row_back = ones_where(
        lax.broadcasted_iota(jnp.int32, (3 * strip, W), 0) == folded((3 * strip, W), 1) + wide(offset, W)
    )

    halo_copy = [
        [remote(halo_out.at[n, s], halo_in.at[1 - n, s], halo_ss.at[n, s], halo_rs.at[1 - n, s], near[n]) for s in range(layers)]
        for n in (0, 1)
    ]
    for n in (0, 1):
        pos_copy[1 - n].wait_recv()
        pick[n] = column_pick(pos_in[n, 1][:1])
    for s in range(layers):
        for n in (0, 1):
            halo_out[n, s] = select_right(v_ref[s], pick[n])
            halo_copy[n][s].start()

    def window_copy(slice_at, sent, depth_at):
        return remote(V.at[slice_at], V.at[slice_at], sent, recv_v.at[slice_at], there(g, depth_at))

    for s in range(layers):
        mine = layers * d + s
        halo_copy[1][s].wait_recv()
        halo_copy[0][s].wait_recv()
        tall = jnp.concatenate([halo_in[0, s], own_cut[s], halo_in[1, s]], axis=0)
        V[mine] = select_left(row_pick, tall)

        @pl.when(jnp.logical_not(active))
        def _():
            window_copy(mine, send_v.at[2, s], partner).start()

        window_copy(mine, send_v.at[0, s], up).start()
        window_copy(mine, send_v.at[1, s], down).start()

    per = 2 * layers

    def gradient_copy(slot):
        return remote(dbuf.at[slot], dbuf.at[slot], send_d.at[slot % 2], recv_d.at[slot % 2], there(g, partner))

    def trans(s, ar, ai):
        c, n = cs[s, 0], cs[s, 1]
        return c * ar - n * ai, c * ai + n * ar

    @pl.when(active)
    def _():
        low, high = (y + 3) % 4, (y + 1) % 4
        first, last = y == 1, y == 3
        steps = [(low * per + j, jnp.where(first, j, (2, 5)[j]), up) for j in (0, 1)]
        steps += [(high * per + j, jnp.where(last, j, (4, 7)[j - 2]), down) for j in (2, 3)]

        def arrive(s):
            for k, (which, when, where) in enumerate(steps):
                @pl.when(s == when)
                def _():
                    window_copy(which, relay_s.at[k], where).wait_recv()
                    window_copy(which, relay_s.at[k], where).start()

            passed_on = ((s // per == low) & (s % per < 2)) | ((s // per == high) & (s % per >= 2))

            @pl.when((s // layers != d) & jnp.logical_not(passed_on))
            def _():
                window_copy(s, relay_s.at[0], partner).wait_recv()

        def enter(s):
            c, n = sincos(V[s])
            cs[s, 0] = c
            cs[s, 1] = n
            ar, ai = ps[0], ps[1]
            ur, ui = c * ar - n * ai, c * ai + n * ar

            @pl.when(s // per == y)
            def _():
                us[s % per, 0] = ur
                us[s % per, 1] = ui

            return ur, ui

        def leave(s, qr, qi):
            @pl.when(s // per == y)
            def _():
                slot = s % per
                dbuf[slot] = -0.5 * (qr * us[slot, 1] + qi * us[slot, 0])

                @pl.when(slot // layers != xl)
                def _():
                    gradient_copy(slot).start()

        @pl.loop(0, slices - 1)
        def _(s):
            arrive(s)
            ur, ui = enter(s)
            ps[0], ps[1] = propagate(ur, ui, T)

        arrive(slices - 1)
        ur, ui = enter(slices - 1)
        qr, qi = detector(ur, ui, i_ref[0], Fr)
        ps[0] = qr
        ps[1] = qi
        leave(slices - 1, qr, qi)

        @pl.loop(0, slices - 1 - per * y)
        def _(t):
            s = slices - 2 - t
            gr, gi = trans(s + 1, ps[0], ps[1])
            qr, qi = propagate(gr, gi, T)
            ps[0] = qr
            ps[1] = qi
            leave(s, qr, qi)

    dep_copy = [
        [remote(dep_out.at[n, s], dep_in.at[1 - n, s], dep_ss.at[n, s], dep_rs.at[1 - n, s], near[n]) for s in range(layers)]
        for n in (0, 1)
    ]
    for s in (1, 0):
        slot = layers * xl + s

        @pl.when(jnp.logical_not(active))
        def _():
            gradient_copy(slot).wait_recv()

        tall = select_left(row_back, dbuf[slot])
        dep_out[0, s] = tall[:strip]
        dep_copy[0][s].start()
        dep_out[1, s] = tall[2 * strip :]
        dep_copy[1][s].start()
        o_ref[s] = spread(tall[strip : 2 * strip], pick[2])
    for s in (1, 0):
        for n in (0, 1):
            dep_copy[1 - n][s].wait_recv()
            o_ref[s] += spread(dep_in[n, s], pick[n])

    for n in (0, 1):
        pos_copy[n].wait_send()
        for s in range(layers):
            halo_copy[n][s].wait_send()
            dep_copy[n][s].wait_send()
    for s in range(layers):
        mine = layers * d + s
        window_copy(mine, send_v.at[0, s], up).wait_send()
        window_copy(mine, send_v.at[1, s], down).wait_send()

    @pl.when(jnp.logical_not(active))
    def _():
        for s in range(layers):
            window_copy(layers * d + s, send_v.at[2, s], partner).wait_send()

    @pl.when(active)
    def _():
        for k in range(4):
            window_copy(0, relay_s.at[k], up).wait_send()
        for s in range(layers):
            gradient_copy(layers * (1 - xl) + s).wait_send()


def local(potential, probe, positions, intensity):
    layers, strip, columns = potential.shape
    groups = lax.axis_size("probe")
    depths = lax.axis_size("depth")
    slices = layers * depths
    T, Fr = tables()
    vm = pl.BlockSpec(memory_space=pltpu.VMEM)
    dma = pltpu.SemaphoreType.DMA
    return pl.pallas_call(
        functools.partial(kernel, groups, depths),
        out_shape=jax.ShapeDtypeStruct(potential.shape, f32),
        in_specs=[vm, vm, pl.BlockSpec(memory_space=pltpu.SMEM), vm, vm, vm],
        out_specs=vm,
        scratch_shapes=[
            pltpu.VMEM((slices, W, W), f32),
            pltpu.VMEM((slices, 2, W, W), f32),
            pltpu.VMEM((2 * layers, 2, W, W), f32),
            pltpu.VMEM((2, W, W), f32),
            pltpu.VMEM((2 * layers, W, W), f32),
            pltpu.VMEM((2, 8, 128), jnp.int32),
            pltpu.VMEM((2, 2, 8, 128), jnp.int32),
            pltpu.VMEM((2, layers, strip, W), f32),
            pltpu.VMEM((2, layers, strip, W), f32),
            pltpu.VMEM((2, layers, strip, W), f32),
            pltpu.VMEM((2, layers, strip, W), f32),
            pltpu.VMEM((layers, strip, W), f32),
            pltpu.VMEM((3, columns, W), bf16),
            dma((2,)), dma((2,)), dma((2, layers)), dma((2, layers)),
            dma((3, layers)), dma((slices,)), dma((4,)), dma((2,)), dma((2,)),
            dma((2, layers)), dma((2, layers)),
        ],
        compiler_params=pltpu.CompilerParams(
            collective_id=0, has_side_effects=True, vmem_limit_bytes=56 << 20
        ),
    )(potential, probe, positions, intensity, jnp.asarray(T), jnp.asarray(Fr))


def solution(mesh):
    in_specs = (P("depth", "probe", None), P(), P("probe", None), P("probe", None, None))
    out_specs = P("depth", "probe", None)
    return jax.shard_map(local, mesh=mesh, in_specs=in_specs, out_specs=out_specs, check_vma=False)
```

```python
import functools

import jax
import jax.numpy as jnp
import ml_dtypes
import numpy as np
from jax import lax
from jax.experimental import pallas as pl
from jax.experimental.pallas import tpu as pltpu
from jax.sharding import PartitionSpec as P
W=256; HB=128
f32=jnp.float32; bf16=jnp.bfloat16

def fit(fn, degree, top):
    n=64
    z=(np.cos(np.pi*(np.arange(n)+.5)/n)+1)*top/2
    return np.polynomial.chebyshev.Chebyshev.fit(z, fn(z), degree, domain=[0,top]).convert(kind=np.polynomial.Polynomial).coef
SINC=fit(lambda z: np.sin(np.sqrt(z))/np.sqrt(z),6,9.0)
COSC=fit(lambda z: np.cos(np.sqrt(z)),6,9.0)

def halves(a):
    hi=a.astype(np.float32).astype(ml_dtypes.bfloat16)
    lo=(a-hi.astype(np.float64)).astype(np.float32).astype(ml_dtypes.bfloat16)
    return hi,lo

def tables():
    k=np.arange(W)
    F=np.exp(-2j*np.pi*((k[:,None]*k[None,:])%W)/W)/np.sqrt(W)
    fr=(((k+W//2)%W)-W//2)/W
    h=np.exp(-60j*fr*fr)
    A=np.conj(F)@np.diag(h)@F
    order=np.concatenate([np.arange(HB), W-1-np.arange(HB)])
    PP=A[:HB,:HB]; Q=A[:HB][:,order[HB:]]
    out=[]
    for B in ((PP+Q)/2,(PP-Q)/2):
        right=np.block([[B.real,B.imag],[-B.imag,B.real]])
        left=np.block([[B.real,-B.imag],[B.imag,B.real]])
        out.append((right,left))
    prop=[out[0][0],out[1][0],out[0][1],out[1][1]]
    G=F[:,order]
    far=[G.T.real,G.T.imag,G.real,G.imag]
    hp,lp=zip(*[halves(a) for a in prop]); hf,lf=zip(*[halves(a) for a in far])
    return np.stack([np.stack(hp),np.stack(lp)]), np.stack([np.stack(hf),np.stack(lf)])

def split(x):
    hi=x.astype(bf16)
    return hi,(x-hi.astype(f32)).astype(bf16)

def dot(a,b):
    return lax.dot_general(a,b,(((1,),(0,)),((),())),preferred_element_type=f32)

def mm_right(x, wh, wl):
    h,l=split(x)
    return dot(h,wh)+dot(l,wh)+dot(h,wl)
def mm_left(wh,wl,x):
    h,l=split(x)
    return dot(wh,h)+dot(wh,l)+dot(wl,h)

def propagate(ur,ui,T):
    ure,uro=ur[:,:HB]+ur[:,HB:],ur[:,:HB]-ur[:,HB:]
    uie,uio=ui[:,:HB]+ui[:,HB:],ui[:,:HB]-ui[:,HB:]
    ye=mm_right(jnp.concatenate([ure,uie],1),T[0,0],T[1,0])
    yo=mm_right(jnp.concatenate([uro,uio],1),T[0,1],T[1,1])
    te,be=ye[:HB]+ye[HB:],ye[:HB]-ye[HB:]
    to,bo=yo[:HB]+yo[HB:],yo[:HB]-yo[HB:]
    re=jnp.concatenate([jnp.concatenate([te[:,:HB],to[:,:HB]],1),jnp.concatenate([te[:,HB:],to[:,HB:]],1)],0)
    ro=jnp.concatenate([jnp.concatenate([be[:,:HB],bo[:,:HB]],1),jnp.concatenate([be[:,HB:],bo[:,HB:]],1)],0)
    ze=mm_left(T[0,2],T[1,2],re)
    zo=mm_left(T[0,3],T[1,3],ro)
    top=ze+zo; bot=ze-zo
    def unfold(t,b):
        return jnp.concatenate([jnp.concatenate([t[:,:HB]+t[:,HB:],t[:,:HB]-t[:,HB:]],1),
                                jnp.concatenate([b[:,:HB]+b[:,HB:],b[:,:HB]-b[:,HB:]],1)],0)
    return unfold(top[:HB],bot[:HB]),unfold(top[HB:],bot[HB:])

def cmm_right(xr,xi,rh,rl,ih,il):
    hr,lr=split(xr); hi,li=split(xi)
    yr=dot(hr,rh)+dot(lr,rh)+dot(hr,rl)-(dot(hi,ih)+dot(li,ih)+dot(hi,il))
    yi=dot(hr,ih)+dot(lr,ih)+dot(hr,il)+(dot(hi,rh)+dot(li,rh)+dot(hi,rl))
    return yr,yi
def cmm_left(rh,rl,ih,il,xr,xi):
    hr,lr=split(xr); hi,li=split(xi)
    yr=dot(rh,hr)+dot(rh,lr)+dot(rl,hr)-(dot(ih,hi)+dot(ih,li)+dot(il,hi))
    yi=dot(ih,hr)+dot(ih,lr)+dot(il,hr)+(dot(rh,hi)+dot(rh,li)+dot(rl,hi))
    return yr,yi

def poly(c,z):
    r=jnp.full_like(z,float(c[-1]))
    for a in c[-2::-1]:
        r=r*z+float(a)
    return r
def sincos(v):
    x=0.5*v; z=x*x
    return poly(COSC,z), x*poly(SINC,z)

def detector(ur,ui,inten,Fr):
    yr,yi=cmm_right(ur,ui,Fr[0,0],Fr[1,0],Fr[0,1],Fr[1,1])
    fr,fi=cmm_left(Fr[0,2],Fr[1,2],Fr[0,3],Fr[1,3],yr,yi)
    m=fr*fr+fi*fi-inten
    gr,gi=m*fr,-(m*fi)
    yr,yi=cmm_right(gr,gi,Fr[0,2],Fr[1,2],Fr[0,3],Fr[1,3])
    return cmm_left(Fr[0,0],Fr[1,0],Fr[0,1],Fr[1,1],yr,yi)


def exact_parts(x):
    high = x.astype(bf16)
    rest = x - high.astype(f32)
    mid = rest.astype(bf16)
    return high, mid, (rest - mid.astype(f32)).astype(bf16)


def select_right(x, chosen):
    a, b, c = exact_parts(x)
    return dot(a, chosen) + dot(b, chosen) + dot(c, chosen)


def select_left(chosen, x):
    a, b, c = exact_parts(x)
    return dot(chosen, a) + dot(chosen, b) + dot(chosen, c)


def spread(x, chosen):
    return sum(
        lax.dot_general(part, chosen, (((1,), (1,)), ((), ())), preferred_element_type=f32)
        for part in exact_parts(x)
    )


def folded(shape, dim):
    index = lax.broadcasted_iota(jnp.int32, shape, dim)
    return jnp.where(index < HB, index, W + HB - 1 - index)


def ones_where(condition):
    return jnp.where(condition, 1.0, 0.0).astype(bf16)


def wide(row, width):
    return jnp.concatenate([row] * (width // 128), axis=1)


def kernel(
    groups, depths, v_ref, p_ref, pos_ref, i_ref, T, Fr, o_ref,
    V, held, cs, us, ps, pos_out, pos_in, halo_out, halo_in, dep_out, dep_mid, dep_in, own_cut, pick,
    pos_ss, pos_rs, halo_ss, halo_rs, send_v, recv_v, held_s, held_r, dep_ss, dep_rs, mid_s, mid_r,
):
    layers, strip, columns = v_ref.shape
    slices = layers * depths
    rows = groups * strip
    g = lax.axis_index("probe")
    d = lax.axis_index("depth")
    y = d // 2
    xl = d % 2
    core = g % 2
    active = xl == core
    before, after = (g + groups - 1) % groups, (g + 1) % groups
    beside = g + 1 - 2 * core
    partner = d + 1 - 2 * xl
    up, down = (d + 2) % depths, (d + depths - 2) % depths

    def there(probe_at, depth_at):
        return {"probe": probe_at, "depth": depth_at}

    barrier = pltpu.get_barrier_semaphore()
    peers = [there(near_by, at) for near_by in (before, after) for at in (d, partner)]
    peers += [there(g, partner)]
    peers += [there(near_by, at) for near_by in (g, beside) for at in (up, down)]
    for peer in peers:
        pl.semaphore_signal(barrier, inc=1, device_id=peer, device_id_type=pl.DeviceIdType.MESH)
    pos_out[0] = jnp.full((8, 128), pos_ref[0, 0], jnp.int32)
    pos_out[1] = jnp.full((8, 128), pos_ref[0, 1], jnp.int32)
    pl.semaphore_wait(barrier, len(peers))

    def remote(source, target, sent, received, where):
        return pltpu.make_async_remote_copy(
            src_ref=source, dst_ref=target, send_sem=sent, recv_sem=received,
            device_id=where, device_id_type=pl.DeviceIdType.MESH,
        )

    near = (there(before, d), there(after, d))
    pos_copy = [remote(pos_out, pos_in.at[1 - n], pos_ss.at[n], pos_rs.at[1 - n], near[n]) for n in (0, 1)]
    for n in (0, 1):
        pos_copy[n].start()

    lines = lax.broadcasted_iota(jnp.int32, (columns, W), 0)
    place = folded((columns, W), 1)

    def column_pick(left):
        return ones_where(lines == place + wide(left, W))

    pick[2] = column_pick(pos_out[1][:1])
    for s in range(layers):
        own_cut[s] = select_right(v_ref[s], pick[2])
    fold = ones_where(lax.broadcasted_iota(jnp.int32, (W, W), 0) == folded((W, W), 1))
    for c in (0, 1):
        ps[c] = select_left(fold, select_right(p_ref[c], fold))
    offset = (pos_out[0][:1] - (g - 1) * strip + rows) & (rows - 1)
    row_pick = ones_where(
        lax.broadcasted_iota(jnp.int32, (W, 3 * strip), 1) == folded((W, 3 * strip), 0) + wide(offset, 3 * strip)
    )
    row_back = ones_where(
        lax.broadcasted_iota(jnp.int32, (3 * strip, W), 0) == folded((3 * strip, W), 1) + wide(offset, W)
    )

    halo_copy = [
        [remote(halo_out.at[n, s], halo_in.at[1 - n, s], halo_ss.at[n, s], halo_rs.at[1 - n, s], near[n]) for s in range(layers)]
        for n in (0, 1)
    ]
    for n in (0, 1):
        pos_copy[1 - n].wait_recv()
        pick[n] = column_pick(pos_in[n, 1][:1])
    for s in range(layers):
        for n in (0, 1):
            halo_out[n, s] = select_right(v_ref[s], pick[n])
            halo_copy[n][s].start()

    def into_window(source, slice_at, sent, probe_at, depth_at):
        return remote(source, V.at[slice_at], sent, recv_v.at[slice_at], there(probe_at, depth_at))

    def into_held(source, k, sent, probe_at, depth_at):
        return remote(source, held.at[k], sent, held_r.at[k], there(probe_at, depth_at))

    def own_sends(s):
        mine = layers * d + s
        if s == 0:
            return (
                into_held(V.at[mine], 2, send_v.at[s, 0], beside, up),
                into_window(V.at[mine], mine, send_v.at[s, 1], g, down),
            )
        return (
            into_window(V.at[mine], mine, send_v.at[s, 0], g, up),
            into_held(V.at[mine], 4, send_v.at[s, 1], beside, down),
        )

    def other_send(s):
        return into_held(V.at[layers * d + s], s, send_v.at[s, 0], beside, partner)

    for s in range(layers):
        mine = layers * d + s
        halo_copy[1][s].wait_recv()
        halo_copy[0][s].wait_recv()
        tall = jnp.concatenate([halo_in[0, s], own_cut[s], halo_in[1, s]], axis=0)
        V[mine] = select_left(row_pick, tall)

        @pl.when(active)
        def _():
            for copy in own_sends(s):
                copy.start()

        @pl.when(jnp.logical_not(active))
        def _():
            other_send(s).start()

    per = 2 * layers

    def passing():
        low, high = (partner + depths - 2) % depths, (partner + 2) % depths

        def sends(k, slice_at, *targets):
            out = [into_window(held.at[k], slice_at, held_s.at[k, 0], beside, d)]
            for n, (what, where) in enumerate(targets):
                if what is None:
                    out.append(into_window(held.at[k], slice_at, held_s.at[k, n + 1], beside, where))
                else:
                    out.append(into_held(held.at[k], what, held_s.at[k, n + 1], g, where))
            return k, out

        return (
            sends(0, layers * partner, (3, up), (None, down)),
            sends(2, layers * down, (None, up)),
            sends(4, layers * up + 1, (None, down)),
            sends(1, layers * partner + 1, (None, up), (5, down)),
            sends(3, layers * low, (None, up)),
            sends(5, layers * high + 1, (None, down)),
        )

    @pl.when(jnp.logical_not(active))
    def _():
        for k, copies in passing():
            into_held(held.at[k], k, held_s.at[k, 0], beside, d).wait_recv()
            for copy in copies:
                copy.start()

    def edge_copy(n, slot):
        return remote(
            dep_out.at[n, slot], dep_in.at[1 - n, slot % layers], dep_ss.at[n, slot],
            dep_rs.at[1 - n, slot % layers], there((before, after)[n], 2 * y + slot // layers),
        )

    def middle_copy(slot):
        return remote(dep_mid.at[slot], dep_mid.at[slot], mid_s.at[slot % layers], mid_r.at[slot % layers], there(g, partner))

    def trans(s, ar, ai):
        c, n = cs[s, 0], cs[s, 1]
        return c * ar - n * ai, c * ai + n * ar

    @pl.when(active)
    def _():
        def arrive(s):
            @pl.when(s // layers != d)
            def _():
                into_window(V.at[s], s, send_v.at[0, 0], g, partner).wait_recv()

        def enter(s):
            c, n = sincos(V[s])
            cs[s, 0] = c
            cs[s, 1] = n
            ar, ai = ps[0], ps[1]
            ur, ui = c * ar - n * ai, c * ai + n * ar

            @pl.when(s // per == y)
            def _():
                us[s % per, 0] = ur
                us[s % per, 1] = ui

            return ur, ui

        def leave(s, qr, qi):
            @pl.when(s // per == y)
            def _():
                slot = s % per
                tall = select_left(row_back, -0.5 * (qr * us[slot, 1] + qi * us[slot, 0]))
                dep_out[0, slot] = tall[:strip]
                edge_copy(0, slot).start()
                dep_out[1, slot] = tall[2 * strip :]
                edge_copy(1, slot).start()
                dep_mid[slot] = tall[strip : 2 * strip]

                @pl.when(slot // layers != xl)
                def _():
                    middle_copy(slot).start()

        @pl.loop(0, slices - 1)
        def _(s):
            arrive(s)
            ur, ui = enter(s)
            ps[0], ps[1] = propagate(ur, ui, T)

        arrive(slices - 1)
        ur, ui = enter(slices - 1)
        qr, qi = detector(ur, ui, i_ref[0], Fr)
        ps[0] = qr
        ps[1] = qi
        leave(slices - 1, qr, qi)

        @pl.loop(0, slices - 1 - per * y)
        def _(t):
            s = slices - 2 - t
            gr, gi = trans(s + 1, ps[0], ps[1])
            qr, qi = propagate(gr, gi, T)
            ps[0] = qr
            ps[1] = qi
            leave(s, qr, qi)

    for s in (1, 0):
        slot = layers * xl + s

        @pl.when(jnp.logical_not(active))
        def _():
            middle_copy(slot).wait_recv()

        total = spread(dep_mid[slot], pick[2])
        for n in (0, 1):
            edge_copy(1 - n, slot).wait_recv()
            total += spread(dep_in[n, s], pick[n])
        o_ref[s] = total

    for n in (0, 1):
        pos_copy[n].wait_send()
        for s in range(layers):
            halo_copy[n][s].wait_send()

    @pl.when(jnp.logical_not(active))
    def _():
        for s in range(layers):
            other_send(s).wait_send()
        for k, copies in passing():
            for copy in copies:
                copy.wait_send()

    @pl.when(active)
    def _():
        for s in range(layers):
            for copy in own_sends(s):
                copy.wait_send()
            middle_copy(layers * (1 - xl) + s).wait_send()
        for slot in range(per):
            for n in (0, 1):
                edge_copy(n, slot).wait_send()


def local(potential, probe, positions, intensity):
    layers, strip, columns = potential.shape
    groups = lax.axis_size("probe")
    depths = lax.axis_size("depth")
    slices = layers * depths
    T, Fr = tables()
    vm = pl.BlockSpec(memory_space=pltpu.VMEM)
    dma = pltpu.SemaphoreType.DMA
    return pl.pallas_call(
        functools.partial(kernel, groups, depths),
        out_shape=jax.ShapeDtypeStruct(potential.shape, f32),
        in_specs=[vm, vm, pl.BlockSpec(memory_space=pltpu.SMEM), vm, vm, vm],
        out_specs=vm,
        scratch_shapes=[
            pltpu.VMEM((slices, W, W), f32),
            pltpu.VMEM((6, W, W), f32),
            pltpu.VMEM((slices, 2, W, W), f32),
            pltpu.VMEM((2 * layers, 2, W, W), f32),
            pltpu.VMEM((2, W, W), f32),
            pltpu.VMEM((2, 8, 128), jnp.int32),
            pltpu.VMEM((2, 2, 8, 128), jnp.int32),
            pltpu.VMEM((2, layers, strip, W), f32),
            pltpu.VMEM((2, layers, strip, W), f32),
            pltpu.VMEM((2, 2 * layers, strip, W), f32),
            pltpu.VMEM((2 * layers, strip, W), f32),
            pltpu.VMEM((2, layers, strip, W), f32),
            pltpu.VMEM((layers, strip, W), f32),
            pltpu.VMEM((3, columns, W), bf16),
            dma((2,)), dma((2,)), dma((2, layers)), dma((2, layers)),
            dma((layers, 2)), dma((slices,)), dma((6, 3)), dma((6,)),
            dma((2, 2 * layers)), dma((2, layers)), dma((layers,)), dma((layers,)),
        ],
        compiler_params=pltpu.CompilerParams(
            collective_id=0, has_side_effects=True, vmem_limit_bytes=56 << 20
        ),
    )(potential, probe, positions, intensity, jnp.asarray(T), jnp.asarray(Fr))


def solution(mesh):
    in_specs = (P("depth", "probe", None), P(), P("probe", None), P("probe", None, None))
    out_specs = P("depth", "probe", None)
    return jax.shard_map(local, mesh=mesh, in_specs=in_specs, out_specs=out_specs, check_vma=False)
```

```python
import functools

import jax
import jax.numpy as jnp
import ml_dtypes
import numpy as np
from jax import lax
from jax.experimental import pallas as pl
from jax.experimental.pallas import tpu as pltpu
from jax.sharding import PartitionSpec as P
W=256; HB=128
f32=jnp.float32; bf16=jnp.bfloat16

def fit(fn, degree, top):
    n=64
    z=(np.cos(np.pi*(np.arange(n)+.5)/n)+1)*top/2
    return np.polynomial.chebyshev.Chebyshev.fit(z, fn(z), degree, domain=[0,top]).convert(kind=np.polynomial.Polynomial).coef
SINC=fit(lambda z: np.sin(np.sqrt(z))/np.sqrt(z),6,9.0)
COSC=fit(lambda z: np.cos(np.sqrt(z)),6,9.0)

def halves(a):
    hi=a.astype(np.float32).astype(ml_dtypes.bfloat16)
    lo=(a-hi.astype(np.float64)).astype(np.float32).astype(ml_dtypes.bfloat16)
    return hi,lo

def tables():
    k=np.arange(W)
    F=np.exp(-2j*np.pi*((k[:,None]*k[None,:])%W)/W)/np.sqrt(W)
    fr=(((k+W//2)%W)-W//2)/W
    h=np.exp(-60j*fr*fr)
    A=np.conj(F)@np.diag(h)@F
    order=np.concatenate([np.arange(HB), W-1-np.arange(HB)])
    PP=A[:HB,:HB]; Q=A[:HB][:,order[HB:]]
    out=[]
    for B in ((PP+Q)/2,(PP-Q)/2):
        right=np.block([[B.real,B.imag],[-B.imag,B.real]])
        left=np.block([[B.real,-B.imag],[B.imag,B.real]])
        out.append((right,left))
    prop=[out[0][0],out[1][0],out[0][1],out[1][1]]
    G=F[:,order]
    far=[G.T.real,G.T.imag,G.real,G.imag]
    hp,lp=zip(*[halves(a) for a in prop]); hf,lf=zip(*[halves(a) for a in far])
    return np.stack([np.stack(hp),np.stack(lp)]), np.stack([np.stack(hf),np.stack(lf)])

def split(x):
    hi=x.astype(bf16)
    return hi,(x-hi.astype(f32)).astype(bf16)

def dot(a,b):
    return lax.dot_general(a,b,(((1,),(0,)),((),())),preferred_element_type=f32)

def mm_right(x, wh, wl):
    h,l=split(x)
    return dot(h,wh)+dot(l,wh)+dot(h,wl)
def mm_left(wh,wl,x):
    h,l=split(x)
    return dot(wh,h)+dot(wh,l)+dot(wl,h)

def propagate(ur,ui,T):
    ure,uro=ur[:,:HB]+ur[:,HB:],ur[:,:HB]-ur[:,HB:]
    uie,uio=ui[:,:HB]+ui[:,HB:],ui[:,:HB]-ui[:,HB:]
    ye=mm_right(jnp.concatenate([ure,uie],1),T[0,0],T[1,0])
    yo=mm_right(jnp.concatenate([uro,uio],1),T[0,1],T[1,1])
    te,be=ye[:HB]+ye[HB:],ye[:HB]-ye[HB:]
    to,bo=yo[:HB]+yo[HB:],yo[:HB]-yo[HB:]
    re=jnp.concatenate([jnp.concatenate([te[:,:HB],to[:,:HB]],1),jnp.concatenate([te[:,HB:],to[:,HB:]],1)],0)
    ro=jnp.concatenate([jnp.concatenate([be[:,:HB],bo[:,:HB]],1),jnp.concatenate([be[:,HB:],bo[:,HB:]],1)],0)
    ze=mm_left(T[0,2],T[1,2],re)
    zo=mm_left(T[0,3],T[1,3],ro)
    top=ze+zo; bot=ze-zo
    def unfold(t,b):
        return jnp.concatenate([jnp.concatenate([t[:,:HB]+t[:,HB:],t[:,:HB]-t[:,HB:]],1),
                                jnp.concatenate([b[:,:HB]+b[:,HB:],b[:,:HB]-b[:,HB:]],1)],0)
    return unfold(top[:HB],bot[:HB]),unfold(top[HB:],bot[HB:])

def cmm_right(xr,xi,rh,rl,ih,il):
    hr,lr=split(xr); hi,li=split(xi)
    yr=dot(hr,rh)+dot(lr,rh)+dot(hr,rl)-(dot(hi,ih)+dot(li,ih)+dot(hi,il))
    yi=dot(hr,ih)+dot(lr,ih)+dot(hr,il)+(dot(hi,rh)+dot(li,rh)+dot(hi,rl))
    return yr,yi
def cmm_left(rh,rl,ih,il,xr,xi):
    hr,lr=split(xr); hi,li=split(xi)
    yr=dot(rh,hr)+dot(rh,lr)+dot(rl,hr)-(dot(ih,hi)+dot(ih,li)+dot(il,hi))
    yi=dot(ih,hr)+dot(ih,lr)+dot(il,hr)+(dot(rh,hi)+dot(rh,li)+dot(rl,hi))
    return yr,yi

def poly(c,z):
    r=jnp.full_like(z,float(c[-1]))
    for a in c[-2::-1]:
        r=r*z+float(a)
    return r
def sincos(v):
    x=0.5*v; z=x*x
    return poly(COSC,z), x*poly(SINC,z)

def detector(ur,ui,inten,Fr):
    yr,yi=cmm_right(ur,ui,Fr[0,0],Fr[1,0],Fr[0,1],Fr[1,1])
    fr,fi=cmm_left(Fr[0,2],Fr[1,2],Fr[0,3],Fr[1,3],yr,yi)
    m=fr*fr+fi*fi-inten
    gr,gi=m*fr,-(m*fi)
    yr,yi=cmm_right(gr,gi,Fr[0,2],Fr[1,2],Fr[0,3],Fr[1,3])
    return cmm_left(Fr[0,0],Fr[1,0],Fr[0,1],Fr[1,1],yr,yi)


def select_right(x, chosen):
    high, low = split(x)
    return dot(high, chosen) + dot(low, chosen)


def select_left(chosen, x):
    high, low = split(x)
    return dot(chosen, high) + dot(chosen, low)


def spread(x, chosen):
    return sum(
        lax.dot_general(part, chosen, (((1,), (1,)), ((), ())), preferred_element_type=f32)
        for part in split(x)
    )


def folded(shape, dim):
    index = lax.broadcasted_iota(jnp.int32, shape, dim)
    return jnp.where(index < HB, index, W + HB - 1 - index)


def ones_where(condition):
    return jnp.where(condition, 1.0, 0.0).astype(bf16)


def wide(row, width):
    return jnp.concatenate([row] * (width // 128), axis=1)


def kernel(
    groups, depths, v_hbm, p_hbm, pos_ref, i_hbm, T_hbm, Fr_hbm, o_ref,
    V, held, wave_in, wave_out, cs, us, ps, pos_out, pos_in, halo_out, halo_in, dep_out, dep_mid, dep_in, own_cut, pick,
    pos_ss, pos_rs, halo_ss, halo_rs, send_v, recv_v, held_s, held_r, dep_ss, dep_rs, mid_s, mid_r, wave_s, wave_r, v_ref, p_ref, i_ref, T, Fr, load_s,
):
    layers, strip, columns = v_hbm.shape
    slices = layers * depths
    rows = groups * strip
    g = lax.axis_index("probe")
    d = lax.axis_index("depth")
    y = d // 2
    xl = d % 2
    core = g % 2
    active = xl == core
    before, after = (g + groups - 1) % groups, (g + 1) % groups
    beside = g + 1 - 2 * core
    partner = d + 1 - 2 * xl
    up, down = (d + 2) % depths, (d + depths - 2) % depths

    def there(probe_at, depth_at):
        return {"probe": probe_at, "depth": depth_at}

    barrier = pltpu.get_barrier_semaphore()
    peers = [there(near_by, at) for near_by in (before, after) for at in (d, partner)]
    peers += [there(g, partner)]
    peers += [there(near_by, at) for near_by in (g, beside) for at in (up, down)]
    across = (d + depths // 2) % depths
    peers += [there(g, across)]
    for peer in peers:
        pl.semaphore_signal(barrier, inc=1, device_id=peer, device_id_type=pl.DeviceIdType.MESH)
    loads = [
        pltpu.make_async_copy(source, target, load_s.at[k])
        for k, (source, target) in enumerate(
            [(v_hbm, v_ref), (p_hbm, p_ref), (i_hbm, i_ref), (T_hbm, T), (Fr_hbm, Fr)]
        )
    ]
    for load in loads:
        load.start()
    pos_out[0] = jnp.full((8, 128), pos_ref[0, 0], jnp.int32)
    pos_out[1] = jnp.full((8, 128), pos_ref[0, 1], jnp.int32)
    pl.semaphore_wait(barrier, len(peers))

    def remote(source, target, sent, received, where):
        return pltpu.make_async_remote_copy(
            src_ref=source, dst_ref=target, send_sem=sent, recv_sem=received,
            device_id=where, device_id_type=pl.DeviceIdType.MESH,
        )

    near = (there(before, d), there(after, d))
    pos_copy = [remote(pos_out, pos_in.at[1 - n], pos_ss.at[n], pos_rs.at[1 - n], near[n]) for n in (0, 1)]
    for n in (0, 1):
        pos_copy[n].start()

    lines = lax.broadcasted_iota(jnp.int32, (columns, W), 0)
    place = folded((columns, W), 1)

    def column_pick(left):
        return ones_where(lines == place + wide(left, W))

    pick[2] = column_pick(pos_out[1][:1])
    for load in loads:
        load.wait()
    for s in range(layers):
        own_cut[s] = select_right(v_ref[s], pick[2])
    fold = ones_where(lax.broadcasted_iota(jnp.int32, (W, W), 0) == folded((W, W), 1))
    for c in (0, 1):
        ps[c] = select_left(fold, select_right(p_ref[c], fold))
    offset = (pos_out[0][:1] - (g - 1) * strip + rows) & (rows - 1)
    row_pick = ones_where(
        lax.broadcasted_iota(jnp.int32, (W, 3 * strip), 1) == folded((W, 3 * strip), 0) + wide(offset, 3 * strip)
    )
    row_back = ones_where(
        lax.broadcasted_iota(jnp.int32, (3 * strip, W), 0) == folded((3 * strip, W), 1) + wide(offset, W)
    )

    halo_copy = [
        [remote(halo_out.at[n, s], halo_in.at[1 - n, s], halo_ss.at[n, s], halo_rs.at[1 - n, s], near[n]) for s in range(layers)]
        for n in (0, 1)
    ]
    for n in (0, 1):
        pos_copy[1 - n].wait_recv()
        pick[n] = column_pick(pos_in[n, 1][:1])
    for s in range(layers):
        for n in (0, 1):
            halo_out[n, s] = select_right(v_ref[s], pick[n])
            halo_copy[n][s].start()

    def into_window(source, slice_at, sent, probe_at, depth_at):
        return remote(source, V.at[slice_at], sent, recv_v.at[slice_at], there(probe_at, depth_at))

    def into_held(source, k, sent, probe_at, depth_at):
        return remote(source, held.at[k], sent, held_r.at[k], there(probe_at, depth_at))

    def needs(target, group):
        target, group = (target + 4) % 4, (group + 4) % 4
        return (target < 2) | ((target == 2) & (group == 3))

    def own_sends(s):
        mine = layers * d + s
        if s == 0:
            return (
                (needs(y + 2, y), into_held(V.at[mine], 2, send_v.at[s, 0], beside, up)),
                (needs(y + 1, y) & ~needs(y + 2, y), into_window(V.at[mine], mine, send_v.at[s, 0], g, up)),
                (needs(y - 1, y), into_window(V.at[mine], mine, send_v.at[s, 1], g, down)),
            )
        return (
            (needs(y - 2, y), into_held(V.at[mine], 4, send_v.at[s, 1], beside, down)),
            (needs(y - 1, y) & ~needs(y - 2, y), into_window(V.at[mine], mine, send_v.at[s, 1], g, down)),
            (needs(y + 1, y), into_window(V.at[mine], mine, send_v.at[s, 0], g, up)),
        )

    def other_send(s):
        return into_held(V.at[layers * d + s], s, send_v.at[s, 0], beside, partner)

    def start_each(pairs):
        for condition, copy in pairs:
            pl.when(condition)(copy.start)

    def end_each(pairs):
        for condition, copy in pairs:
            pl.when(condition)(copy.wait_send)

    for s in range(layers):
        mine = layers * d + s
        halo_copy[1][s].wait_recv()
        halo_copy[0][s].wait_recv()
        tall = jnp.concatenate([halo_in[0, s], own_cut[s], halo_in[1, s]], axis=0)
        V[mine] = select_left(row_pick, tall)

        @pl.when(active)
        def _():
            copies = own_sends(s)
            if s == 0:
                start_each(copies[:2])
                pl.when(copies[2][0] & (y != 2))(copies[2][1].start)
            else:
                start_each(copies)

                @pl.when(y == 2)
                def _():
                    copies[0][1].wait_send()
                    own_sends(0)[2][1].start()

        @pl.when(jnp.logical_not(active))
        def _():
            other_send(s).start()

    per = 2 * layers

    def passing():
        low, high = (partner + depths - 2) % depths, (partner + 2) % depths

        always = y >= 0

        def home(k, slice_at, condition):
            return condition, into_window(held.at[k], slice_at, held_s.at[k, 0], beside, d)

        def window(k, slice_at, condition, where):
            return condition, into_window(held.at[k], slice_at, held_s.at[k, 1], beside, where)

        def direct(k, slice_at, condition, where):
            return condition, into_window(held.at[k], slice_at, held_s.at[k, 2], beside, where)

        def onward(k, to, condition, where):
            return condition, into_held(held.at[k], to, held_s.at[k, 2], g, where)

        first, second = layers * partner, layers * partner + 1
        to_up, to_down = needs(y + 1, y - 1), needs(y - 1, y + 1)
        here_low, here_high = needs(y, y - 1), needs(y, y + 1)
        own_low, own_high = layers * down, layers * up + 1
        part_low, part_high = layers * low, layers * high + 1
        return (
            (0, always, (
                onward(0, 3, needs(y + 2, y), up), direct(0, first, needs(y + 1, y) & ~needs(y + 2, y), up),
                window(0, first, needs(y - 1, y), down), home(0, first, always))),
            (1, always, (
                onward(1, 5, needs(y - 2, y), down), direct(1, second, needs(y - 1, y) & ~needs(y - 2, y), down),
                window(1, second, needs(y + 1, y), up), home(1, second, always))),
            (2, to_up, (window(2, own_low, to_up, up), home(2, own_low, to_up & here_low))),
            (4, to_down, (window(4, own_high, to_down, down), home(4, own_high, to_down & here_high))),
            (3, to_up, (window(3, part_low, to_up, up), home(3, part_low, to_up & here_low))),
            (5, to_down, (window(5, part_high, to_down, down), home(5, part_high, to_down & here_high))),
        )

    @pl.when(jnp.logical_not(active))
    def _():
        for k, comes, copies in passing():
            @pl.when(comes)
            def _():
                into_held(held.at[k], k, held_s.at[k, 0], beside, d).wait_recv()
                if k == 0:
                    pl.when(copies[2][0] & (y != 2))(copies[2][1].start)
                    pl.when(copies[0][0] & (y != 3))(copies[0][1].start)
                    start_each(copies[1:2] + copies[3:])
                elif k == 1:
                    pl.when(copies[2][0] & (y != 3))(copies[2][1].start)
                    start_each(copies[:2] + copies[3:])
                else:
                    start_each(copies)

                if k == 3:
                    @pl.when(y == 3)
                    def _():
                        copies[0][1].wait_send()
                        passing()[0][2][0][1].start()
                        passing()[1][2][2][1].start()

            if k == 1:
                @pl.when(y == 2)
                def _():
                    copies[0][1].wait_send()
                    passing()[0][2][2][1].start()

    def edge_copy(n, slot):
        return remote(
            dep_out.at[n, slot], dep_in.at[1 - n, slot % layers], dep_ss.at[n, slot],
            dep_rs.at[1 - n, slot % layers], there((before, after)[n], 2 * y + slot // layers),
        )

    def middle_copy(slot):
        return remote(dep_mid.at[slot], dep_mid.at[slot], mid_s.at[slot % layers], mid_r.at[slot % layers], there(g, partner))

    def trans(s, ar, ai):
        c, n = cs[s, 0], cs[s, 1]
        return c * ar - n * ai, c * ai + n * ar

    @pl.when(active)
    def _():
        def arrive(s):
            @pl.when(s // layers != d)
            def _():
                into_window(V.at[s], s, send_v.at[0, 0], g, partner).wait_recv()

        def prepare(s):
            arrive(s)
            c, n = sincos(V[s])
            cs[s, 0] = c
            cs[s, 1] = n

        ready = jnp.where(y == 0, 0, per * y)
        ready_end = jnp.where(y == 0, 0, jnp.where(y == 2, slices, per * (y + 1)))

        def wave_copy(k, to, where):
            return remote(wave_out.at[k], wave_in.at[to], wave_s.at[k], wave_r.at[to], there(g, where))

        @pl.loop(ready, ready_end)
        def _(s):
            prepare(s)

        @pl.when(y >= 2)
        def _():
            for c in (0, 1):
                wave_copy(c, c, down).wait_recv()
                ps[c] = wave_in[c]

        def enter(s):
            @pl.when((s < ready) | (s >= ready_end))
            def _():
                prepare(s)

            c, n = cs[s, 0], cs[s, 1]
            ar, ai = ps[0], ps[1]
            ur, ui = c * ar - n * ai, c * ai + n * ar

            @pl.when(s // per == y)
            def _():
                us[s % per, 0] = ur
                us[s % per, 1] = ui

            return ur, ui

        def leave(s, qr, qi):
            @pl.when(s // per == y)
            def _():
                slot = s % per
                tall = select_left(row_back, -0.5 * (qr * us[slot, 1] + qi * us[slot, 0]))
                dep_out[0, slot] = tall[:strip]
                edge_copy(0, slot).start()
                dep_out[1, slot] = tall[2 * strip :]
                edge_copy(1, slot).start()
                dep_mid[slot] = tall[strip : 2 * strip]

                @pl.when(slot // layers != xl)
                def _():
                    middle_copy(slot).start()

        @pl.loop(jnp.where(y < 2, 0, per * y), slices - 1)
        def _(s):
            ur, ui = enter(s)
            ps[0], ps[1] = propagate(ur, ui, T)

            @pl.when((y == 1) & (s == 2 * per - 1))
            def _():
                wave_out[0] = ps[0]
                wave_copy(0, 0, up).start()

            @pl.when((y == 0) & (s == 2 * per - 1))
            def _():
                wave_out[0] = ps[1]
                wave_copy(0, 1, across).start()

            @pl.when((y == 0) & (s == 3 * per - 1))
            def _():
                for c in (0, 1):
                    wave_out[1 + c] = ps[c]
                    wave_copy(1 + c, c, down).start()

        ur, ui = enter(slices - 1)
        qr, qi = detector(ur, ui, i_ref[0], Fr)

        @pl.when(y < 2)
        def _():
            wave_copy(0, 0, up).wait_send()

        @pl.when(y == 0)
        def _():
            for c in (0, 1):
                wave_copy(1 + c, c, down).wait_send()

        ps[0] = qr
        ps[1] = qi
        leave(slices - 1, qr, qi)

        @pl.loop(0, slices - 1 - per * y)
        def _(t):
            s = slices - 2 - t
            gr, gi = trans(s + 1, ps[0], ps[1])
            qr, qi = propagate(gr, gi, T)
            ps[0] = qr
            ps[1] = qi
            leave(s, qr, qi)

    for s in (1, 0):
        slot = layers * xl + s

        @pl.when(jnp.logical_not(active))
        def _():
            middle_copy(slot).wait_recv()

        total = spread(dep_mid[slot], pick[2])
        for n in (0, 1):
            edge_copy(1 - n, slot).wait_recv()
            total += spread(dep_in[n, s], pick[n])
        o_ref[s] = total

    for n in (0, 1):
        pos_copy[n].wait_send()
        for s in range(layers):
            halo_copy[n][s].wait_send()

    @pl.when(jnp.logical_not(active))
    def _():
        for s in range(layers):
            other_send(s).wait_send()
        for k, comes, copies in passing():
            if k == 1:
                end_each(copies[1:])
                pl.when(copies[0][0] & (y != 2))(copies[0][1].wait_send)
            elif k == 3:
                end_each(copies[1:])
                pl.when(copies[0][0] & (y != 3))(copies[0][1].wait_send)
            else:
                end_each(copies)

    @pl.when(active)
    def _():
        for s in range(layers):
            copies = own_sends(s)
            if s == 0:
                end_each(copies)
            else:
                end_each(copies[1:])
                pl.when(copies[0][0] & (y != 2))(copies[0][1].wait_send)
            middle_copy(layers * (1 - xl) + s).wait_send()
        for slot in range(per):
            for n in (0, 1):
                edge_copy(n, slot).wait_send()


def local(potential, probe, positions, intensity):
    layers, strip, columns = potential.shape
    groups = lax.axis_size("probe")
    depths = lax.axis_size("depth")
    slices = layers * depths
    T, Fr = tables()
    vm = pl.BlockSpec(memory_space=pltpu.VMEM)
    far = pl.BlockSpec(memory_space=pl.ANY)
    dma = pltpu.SemaphoreType.DMA
    return pl.pallas_call(
        functools.partial(kernel, groups, depths),
        out_shape=jax.ShapeDtypeStruct(potential.shape, f32),
        in_specs=[far, far, pl.BlockSpec(memory_space=pltpu.SMEM), far, far, far],
        out_specs=vm,
        scratch_shapes=[
            pltpu.VMEM((slices, W, W), f32),
            pltpu.VMEM((6, W, W), f32),
            pltpu.VMEM((2, W, W), f32),
            pltpu.VMEM((3, W, W), f32),
            pltpu.VMEM((slices, 2, W, W), f32),
            pltpu.VMEM((2 * layers, 2, W, W), f32),
            pltpu.VMEM((2, W, W), f32),
            pltpu.VMEM((2, 8, 128), jnp.int32),
            pltpu.VMEM((2, 2, 8, 128), jnp.int32),
            pltpu.VMEM((2, layers, strip, W), f32),
            pltpu.VMEM((2, layers, strip, W), f32),
            pltpu.VMEM((2, 2 * layers, strip, W), f32),
            pltpu.VMEM((2 * layers, strip, W), f32),
            pltpu.VMEM((2, layers, strip, W), f32),
            pltpu.VMEM((layers, strip, W), f32),
            pltpu.VMEM((3, columns, W), bf16),
            dma((2,)), dma((2,)), dma((2, layers)), dma((2, layers)),
            dma((layers, 2)), dma((slices,)), dma((6, 3)), dma((6,)),
            dma((2, 2 * layers)), dma((2, layers)), dma((layers,)), dma((layers,)),
            dma((3,)), dma((2,)),
            pltpu.VMEM(potential.shape, f32),
            pltpu.VMEM(probe.shape, f32),
            pltpu.VMEM(intensity.shape, f32),
            pltpu.VMEM(T.shape, bf16),
            pltpu.VMEM(Fr.shape, bf16),
            dma((5,)),
        ],
        compiler_params=pltpu.CompilerParams(
            collective_id=0, has_side_effects=True, vmem_limit_bytes=56 << 20
        ),
    )(potential, probe, positions, intensity, jnp.asarray(T), jnp.asarray(Fr))


def solution(mesh):
    in_specs = (P("depth", "probe", None), P(), P("probe", None), P("probe", None, None))
    out_specs = P("depth", "probe", None)
    return jax.shard_map(local, mesh=mesh, in_specs=in_specs, out_specs=out_specs, check_vma=False)
```

```python
import functools

import jax
import jax.numpy as jnp
import ml_dtypes
import numpy as np
from jax import lax
from jax.experimental import pallas as pl
from jax.experimental.pallas import tpu as pltpu
from jax.sharding import PartitionSpec as P
W=256; HB=128
f32=jnp.float32; bf16=jnp.bfloat16

def fit(fn, degree, top):
    n=64
    z=(np.cos(np.pi*(np.arange(n)+.5)/n)+1)*top/2
    return np.polynomial.chebyshev.Chebyshev.fit(z, fn(z), degree, domain=[0,top]).convert(kind=np.polynomial.Polynomial).coef
SINC=fit(lambda z: np.sin(np.sqrt(z))/np.sqrt(z),6,9.0)
COSC=fit(lambda z: np.cos(np.sqrt(z)),6,9.0)

def halves(a):
    hi=a.astype(np.float32).astype(ml_dtypes.bfloat16)
    lo=(a-hi.astype(np.float64)).astype(np.float32).astype(ml_dtypes.bfloat16)
    return hi,lo

def tables():
    k=np.arange(W)
    F=np.exp(-2j*np.pi*((k[:,None]*k[None,:])%W)/W)/np.sqrt(W)
    fr=(((k+W//2)%W)-W//2)/W
    h=np.exp(-60j*fr*fr)
    A=np.conj(F)@np.diag(h)@F
    order=np.concatenate([np.arange(HB), W-1-np.arange(HB)])
    PP=A[:HB,:HB]; Q=A[:HB][:,order[HB:]]
    out=[]
    for B in ((PP+Q)/2,(PP-Q)/2):
        right=np.block([[B.real,B.imag],[-B.imag,B.real]])
        left=np.block([[B.real,-B.imag],[B.imag,B.real]])
        out.append((right,left))
    prop=[out[0][0],out[1][0],out[0][1],out[1][1]]
    half=np.arange(HB)+.5
    turn=2*np.pi/W*half[:,None]*half[None,:]
    zero=np.zeros((HB,HB))
    waves=np.block([[np.cos(turn),zero],[zero,np.sin(turn)]])/np.sqrt(W)
    shift=np.exp(2j*np.pi*(order/(2*W)+1/(8*W)))
    phase=shift[:,None]*shift[None,:]
    hp,lp=zip(*[halves(a) for a in prop])
    return (np.stack([np.stack(hp),np.stack(lp)]), np.stack(halves(waves)),
            np.stack([phase.real,phase.imag]).astype(np.float32))

def split(x):
    hi=x.astype(bf16)
    return hi,(x-hi.astype(f32)).astype(bf16)

def dot(a,b):
    return lax.dot_general(a,b,(((1,),(0,)),((),())),preferred_element_type=f32)

def mm_right(x, wh, wl):
    h,l=split(x)
    y=dot(jnp.concatenate([h,l],0),wh)
    return y[:W]+y[W:]+dot(h,wl)
def mm_left(wh,wl,x):
    h,l=split(x)
    y=dot(jnp.concatenate([wh,wl],0),h)
    return y[:W]+y[W:]+dot(wh,l)

def propagate(ur,ui,T):
    ure,uro=ur[:,:HB]+ur[:,HB:],ur[:,:HB]-ur[:,HB:]
    uie,uio=ui[:,:HB]+ui[:,HB:],ui[:,:HB]-ui[:,HB:]
    ye=mm_right(jnp.concatenate([ure,uie],1),T[0,0],T[1,0])
    yo=mm_right(jnp.concatenate([uro,uio],1),T[0,1],T[1,1])
    te,be=ye[:HB]+ye[HB:],ye[:HB]-ye[HB:]
    to,bo=yo[:HB]+yo[HB:],yo[:HB]-yo[HB:]
    re=jnp.concatenate([jnp.concatenate([te[:,:HB],to[:,:HB]],1),jnp.concatenate([te[:,HB:],to[:,HB:]],1)],0)
    ro=jnp.concatenate([jnp.concatenate([be[:,:HB],bo[:,:HB]],1),jnp.concatenate([be[:,HB:],bo[:,HB:]],1)],0)
    ze=mm_left(T[0,2],T[1,2],re)
    zo=mm_left(T[0,3],T[1,3],ro)
    top=ze+zo; bot=ze-zo
    def unfold(t,b):
        return jnp.concatenate([jnp.concatenate([t[:,:HB]+t[:,HB:],t[:,:HB]-t[:,HB:]],1),
                                jnp.concatenate([b[:,:HB]+b[:,HB:],b[:,:HB]-b[:,HB:]],1)],0)
    return unfold(top[:HB],bot[:HB]),unfold(top[HB:],bot[HB:])

def shifted_right(xr,xi,w):
    def parts(x):
        p=mm_right(jnp.concatenate([x[:,:HB]-x[:,HB:],x[:,:HB]+x[:,HB:]],1),w[0],w[1])
        return p[:,:HB],p[:,HB:]
    (ar,br),(ai,bi)=parts(xr),parts(xi)
    return jnp.concatenate([bi+ar,bi-ar],1),jnp.concatenate([ai-br,-ai-br],1)

def shifted_left(w,xr,xi):
    def parts(x):
        p=mm_left(w[0],w[1],jnp.concatenate([x[:HB]-x[HB:],x[:HB]+x[HB:]],0))
        return p[:HB],p[HB:]
    (ar,br),(ai,bi)=parts(xr),parts(xi)
    return jnp.concatenate([bi+ar,bi-ar],0),jnp.concatenate([ai-br,-ai-br],0)

def poly(c,z):
    r=jnp.full_like(z,float(c[-1]))
    for a in c[-2::-1]:
        r=r*z+float(a)
    return r
def sincos(v):
    x=0.5*v; z=x*x
    return poly(COSC,z), x*poly(SINC,z)

def detector(ur,ui,inten,Fr,phase):
    er,ei=phase[0],phase[1]
    yr,yi=shifted_right(er*ur-ei*ui,er*ui+ei*ur,Fr)
    vr,vi=shifted_left(Fr,yr,yi)
    m=vr*vr+vi*vi-inten
    yr,yi=shifted_right(m*vr,-(m*vi),Fr)
    zr,zi=shifted_left(Fr,yr,yi)
    return er*zr-ei*zi,er*zi+ei*zr

def select_right(x, chosen):
    high, low = split(x)
    return dot(high, chosen) + dot(low, chosen)


def select_left(chosen, x):
    high, low = split(x)
    return dot(chosen, high) + dot(chosen, low)


def spread(x, chosen):
    return sum(
        lax.dot_general(part, chosen, (((1,), (1,)), ((), ())), preferred_element_type=f32)
        for part in split(x)
    )


def folded(shape, dim):
    index = lax.broadcasted_iota(jnp.int32, shape, dim)
    return jnp.where(index < HB, index, W + HB - 1 - index)


def ones_where(condition):
    return jnp.where(condition, 1.0, 0.0).astype(bf16)


def wide(row, width):
    return jnp.concatenate([row] * (width // 128), axis=1)


def kernel(
    groups, depths, v_hbm, p_hbm, pos_ref, i_hbm, T_hbm, Fr_hbm, phase_hbm, o_ref,
    V, held, wave_in, wave_out, cs, us, ps, pos_out, pos_in, halo_out, halo_in, dep_out, dep_mid, dep_in, own_cut, pick,
    pos_ss, pos_rs, halo_ss, halo_rs, send_v, recv_v, held_s, held_r, dep_ss, dep_rs, mid_s, mid_r, wave_s, wave_r, v_ref, p_ref, i_ref, T, Fr, phase, load_s,
):
    layers, strip, columns = v_hbm.shape
    slices = layers * depths
    rows = groups * strip
    g = lax.axis_index("probe")
    d = lax.axis_index("depth")
    y = d // 2
    xl = d % 2
    core = g % 2
    active = xl == core
    before, after = (g + groups - 1) % groups, (g + 1) % groups
    beside = g + 1 - 2 * core
    partner = d + 1 - 2 * xl
    up, down = (d + 2) % depths, (d + depths - 2) % depths

    def there(probe_at, depth_at):
        return {"probe": probe_at, "depth": depth_at}

    barrier = pltpu.get_barrier_semaphore()
    peers = [there(near_by, at) for near_by in (before, after) for at in (d, partner)]
    peers += [there(g, partner)]
    peers += [there(near_by, at) for near_by in (g, beside) for at in (up, down)]
    across = (d + depths // 2) % depths
    peers += [there(g, across)]
    for peer in peers:
        pl.semaphore_signal(barrier, inc=1, device_id=peer, device_id_type=pl.DeviceIdType.MESH)
    loads = [
        pltpu.make_async_copy(source, target, load_s.at[k])
        for k, (source, target) in enumerate(
            [(v_hbm, v_ref), (p_hbm, p_ref), (i_hbm, i_ref), (T_hbm, T), (Fr_hbm, Fr), (phase_hbm, phase)]
        )
    ]
    for load in loads:
        load.start()
    pos_out[0] = jnp.full((8, 128), pos_ref[0, 0], jnp.int32)
    pos_out[1] = jnp.full((8, 128), pos_ref[0, 1], jnp.int32)
    pl.semaphore_wait(barrier, len(peers))

    def remote(source, target, sent, received, where):
        return pltpu.make_async_remote_copy(
            src_ref=source, dst_ref=target, send_sem=sent, recv_sem=received,
            device_id=where, device_id_type=pl.DeviceIdType.MESH,
        )

    near = (there(before, d), there(after, d))
    pos_copy = [remote(pos_out, pos_in.at[1 - n], pos_ss.at[n], pos_rs.at[1 - n], near[n]) for n in (0, 1)]
    for n in (0, 1):
        pos_copy[n].start()

    lines = lax.broadcasted_iota(jnp.int32, (columns, W), 0)
    place = folded((columns, W), 1)

    def column_pick(left):
        return ones_where(lines == place + wide(left, W))

    pick[2] = column_pick(pos_out[1][:1])
    for load in loads:
        load.wait()
    for s in range(layers):
        own_cut[s] = select_right(v_ref[s], pick[2])
    fold = ones_where(lax.broadcasted_iota(jnp.int32, (W, W), 0) == folded((W, W), 1))
    for c in (0, 1):
        ps[c] = select_left(fold, select_right(p_ref[c], fold))
    i_ref[0] = select_left(fold, select_right(i_ref[0], fold))
    offset = (pos_out[0][:1] - (g - 1) * strip + rows) & (rows - 1)
    row_pick = ones_where(
        lax.broadcasted_iota(jnp.int32, (W, 3 * strip), 1) == folded((W, 3 * strip), 0) + wide(offset, 3 * strip)
    )
    row_back = ones_where(
        lax.broadcasted_iota(jnp.int32, (3 * strip, W), 0) == folded((3 * strip, W), 1) + wide(offset, W)
    )

    halo_copy = [
        [remote(halo_out.at[n, s], halo_in.at[1 - n, s], halo_ss.at[n, s], halo_rs.at[1 - n, s], near[n]) for s in range(layers)]
        for n in (0, 1)
    ]
    for n in (0, 1):
        pos_copy[1 - n].wait_recv()
        pick[n] = column_pick(pos_in[n, 1][:1])
    for s in range(layers):
        for n in (0, 1):
            halo_out[n, s] = select_right(v_ref[s], pick[n])
            halo_copy[n][s].start()

    def into_window(source, slice_at, sent, probe_at, depth_at):
        return remote(source, V.at[slice_at], sent, recv_v.at[slice_at], there(probe_at, depth_at))

    def into_held(source, k, sent, probe_at, depth_at):
        return remote(source, held.at[k], sent, held_r.at[k], there(probe_at, depth_at))

    def needs(target, group):
        target, group = (target + 4) % 4, (group + 4) % 4
        return (target < 2) | ((target == 2) & (group == 3))

    def own_sends(s):
        mine = layers * d + s
        if s == 0:
            return (
                (needs(y + 2, y), into_held(V.at[mine], 2, send_v.at[s, 0], beside, up)),
                (needs(y + 1, y) & ~needs(y + 2, y), into_window(V.at[mine], mine, send_v.at[s, 0], g, up)),
                (needs(y - 1, y), into_window(V.at[mine], mine, send_v.at[s, 1], g, down)),
            )
        return (
            (needs(y - 2, y), into_held(V.at[mine], 4, send_v.at[s, 1], beside, down)),
            (needs(y - 1, y) & ~needs(y - 2, y), into_window(V.at[mine], mine, send_v.at[s, 1], g, down)),
            (needs(y + 1, y), into_window(V.at[mine], mine, send_v.at[s, 0], g, up)),
        )

    def other_send(s):
        return into_held(V.at[layers * d + s], s, send_v.at[s, 0], beside, partner)

    def start_each(pairs):
        for condition, copy in pairs:
            pl.when(condition)(copy.start)

    def end_each(pairs):
        for condition, copy in pairs:
            pl.when(condition)(copy.wait_send)

    for s in range(layers):
        mine = layers * d + s
        halo_copy[1][s].wait_recv()
        halo_copy[0][s].wait_recv()
        tall = jnp.concatenate([halo_in[0, s], own_cut[s], halo_in[1, s]], axis=0)
        V[mine] = select_left(row_pick, tall)

        @pl.when(active)
        def _():
            copies = own_sends(s)
            if s == 0:
                start_each(copies[:2])
                pl.when(copies[2][0] & (y != 2))(copies[2][1].start)
            else:
                start_each(copies)

                @pl.when(y == 2)
                def _():
                    copies[0][1].wait_send()
                    own_sends(0)[2][1].start()

        @pl.when(jnp.logical_not(active))
        def _():
            other_send(s).start()

    per = 2 * layers

    def passing():
        low, high = (partner + depths - 2) % depths, (partner + 2) % depths

        always = y >= 0

        def home(k, slice_at, condition):
            return condition, into_window(held.at[k], slice_at, held_s.at[k, 0], beside, d)

        def window(k, slice_at, condition, where):
            return condition, into_window(held.at[k], slice_at, held_s.at[k, 1], beside, where)

        def direct(k, slice_at, condition, where):
            return condition, into_window(held.at[k], slice_at, held_s.at[k, 2], beside, where)

        def onward(k, to, condition, where):
            return condition, into_held(held.at[k], to, held_s.at[k, 2], g, where)

        first, second = layers * partner, layers * partner + 1
        to_up, to_down = needs(y + 1, y - 1), needs(y - 1, y + 1)
        here_low, here_high = needs(y, y - 1), needs(y, y + 1)
        own_low, own_high = layers * down, layers * up + 1
        part_low, part_high = layers * low, layers * high + 1
        return (
            (0, always, (
                onward(0, 3, needs(y + 2, y), up), direct(0, first, needs(y + 1, y) & ~needs(y + 2, y), up),
                window(0, first, needs(y - 1, y), down), home(0, first, always))),
            (1, always, (
                onward(1, 5, needs(y - 2, y), down), direct(1, second, needs(y - 1, y) & ~needs(y - 2, y), down),
                window(1, second, needs(y + 1, y), up), home(1, second, always))),
            (2, to_up, (window(2, own_low, to_up, up), home(2, own_low, to_up & here_low))),
            (4, to_down, (window(4, own_high, to_down, down), home(4, own_high, to_down & here_high))),
            (3, to_up, (window(3, part_low, to_up, up), home(3, part_low, to_up & here_low))),
            (5, to_down, (window(5, part_high, to_down, down), home(5, part_high, to_down & here_high))),
        )

    @pl.when(jnp.logical_not(active))
    def _():
        for k, comes, copies in passing():
            @pl.when(comes)
            def _():
                into_held(held.at[k], k, held_s.at[k, 0], beside, d).wait_recv()
                if k == 0:
                    pl.when(copies[2][0] & (y != 2))(copies[2][1].start)
                    pl.when(copies[0][0] & (y != 3))(copies[0][1].start)
                    start_each(copies[1:2] + copies[3:])
                elif k == 1:
                    pl.when(copies[2][0] & (y != 3))(copies[2][1].start)
                    start_each(copies[:2] + copies[3:])
                else:
                    start_each(copies)

                if k == 3:
                    @pl.when(y == 3)
                    def _():
                        copies[0][1].wait_send()
                        passing()[0][2][0][1].start()
                        passing()[1][2][2][1].start()

            if k == 1:
                @pl.when(y == 2)
                def _():
                    copies[0][1].wait_send()
                    passing()[0][2][2][1].start()

    def edge_copy(n, slot):
        return remote(
            dep_out.at[n, slot], dep_in.at[1 - n, slot % layers], dep_ss.at[n, slot],
            dep_rs.at[1 - n, slot % layers], there((before, after)[n], 2 * y + slot // layers),
        )

    def middle_copy(slot):
        return remote(dep_mid.at[slot], dep_mid.at[slot], mid_s.at[slot % layers], mid_r.at[slot % layers], there(g, partner))

    def trans(s, ar, ai):
        c, n = cs[s, 0], cs[s, 1]
        return c * ar - n * ai, c * ai + n * ar

    @pl.when(active)
    def _():
        def arrive(s):
            @pl.when(s // layers != d)
            def _():
                into_window(V.at[s], s, send_v.at[0, 0], g, partner).wait_recv()

        def prepare(s):
            arrive(s)
            c, n = sincos(V[s])
            cs[s, 0] = c
            cs[s, 1] = n

        ready = jnp.where(y == 0, layers * core, per * y)
        ready_end = jnp.where(y == 0, 2 * layers * core, jnp.where(y == 2, slices, per * (y + 1)))

        def wave_copy(k, to, where):
            return remote(wave_out.at[k], wave_in.at[to], wave_s.at[k], wave_r.at[to], there(g, where))

        @pl.loop(ready, ready_end)
        def _(s):
            prepare(s)

        @pl.when(y >= 2)
        def _():
            for c in (0, 1):
                wave_copy(c, c, down).wait_recv()
                ps[c] = wave_in[c]

        def enter(s):
            @pl.when((s < ready) | (s >= ready_end))
            def _():
                prepare(s)

            c, n = cs[s, 0], cs[s, 1]
            ar, ai = ps[0], ps[1]
            ur, ui = c * ar - n * ai, c * ai + n * ar

            @pl.when(s // per == y)
            def _():
                us[s % per, 0] = ur
                us[s % per, 1] = ui

            return ur, ui

        def leave(s, qr, qi):
            @pl.when(s // per == y)
            def _():
                slot = s % per
                tall = select_left(row_back, -0.5 * (qr * us[slot, 1] + qi * us[slot, 0]))
                dep_out[0, slot] = tall[:strip]
                edge_copy(0, slot).start()
                dep_out[1, slot] = tall[2 * strip :]
                edge_copy(1, slot).start()
                dep_mid[slot] = tall[strip : 2 * strip]

                @pl.when(slot // layers != xl)
                def _():
                    middle_copy(slot).start()

        @pl.loop(jnp.where(y < 2, 0, per * y), slices - 1)
        def _(s):
            ur, ui = enter(s)
            ps[0], ps[1] = propagate(ur, ui, T)

            @pl.when((y == 1) & (s == 2 * per - 1))
            def _():
                wave_out[0] = ps[0]
                wave_copy(0, 0, up).start()

            @pl.when((y == 0) & (s == 2 * per - 1))
            def _():
                wave_out[0] = ps[1]
                wave_copy(0, 1, across).start()

            @pl.when((y == 0) & (s == 3 * per - 1))
            def _():
                for c in (0, 1):
                    wave_out[1 + c] = ps[c]
                    wave_copy(1 + c, c, down).start()

        ur, ui = enter(slices - 1)
        qr, qi = detector(ur, ui, i_ref[0], Fr, phase)

        @pl.when(y < 2)
        def _():
            wave_copy(0, 0, up).wait_send()

        @pl.when(y == 0)
        def _():
            for c in (0, 1):
                wave_copy(1 + c, c, down).wait_send()

        ps[0] = qr
        ps[1] = qi
        leave(slices - 1, qr, qi)

        @pl.loop(0, slices - 1 - per * y)
        def _(t):
            s = slices - 2 - t
            gr, gi = trans(s + 1, ps[0], ps[1])
            qr, qi = propagate(gr, gi, T)
            ps[0] = qr
            ps[1] = qi
            leave(s, qr, qi)

    for s in (1, 0):
        slot = layers * xl + s

        @pl.when(jnp.logical_not(active))
        def _():
            middle_copy(slot).wait_recv()

        total = spread(dep_mid[slot], pick[2])
        for n in (0, 1):
            edge_copy(1 - n, slot).wait_recv()
            total += spread(dep_in[n, s], pick[n])
        o_ref[s] = total

    for n in (0, 1):
        pos_copy[n].wait_send()
        for s in range(layers):
            halo_copy[n][s].wait_send()

    @pl.when(jnp.logical_not(active))
    def _():
        for s in range(layers):
            other_send(s).wait_send()
        for k, comes, copies in passing():
            if k == 1:
                end_each(copies[1:])
                pl.when(copies[0][0] & (y != 2))(copies[0][1].wait_send)
            elif k == 3:
                end_each(copies[1:])
                pl.when(copies[0][0] & (y != 3))(copies[0][1].wait_send)
            else:
                end_each(copies)

    @pl.when(active)
    def _():
        for s in range(layers):
            copies = own_sends(s)
            if s == 0:
                end_each(copies)
            else:
                end_each(copies[1:])
                pl.when(copies[0][0] & (y != 2))(copies[0][1].wait_send)
            middle_copy(layers * (1 - xl) + s).wait_send()
        for slot in range(per):
            for n in (0, 1):
                edge_copy(n, slot).wait_send()


def local(potential, probe, positions, intensity):
    layers, strip, columns = potential.shape
    groups = lax.axis_size("probe")
    depths = lax.axis_size("depth")
    slices = layers * depths
    T, Fr, phase = tables()
    vm = pl.BlockSpec(memory_space=pltpu.VMEM)
    far = pl.BlockSpec(memory_space=pl.ANY)
    dma = pltpu.SemaphoreType.DMA
    return pl.pallas_call(
        functools.partial(kernel, groups, depths),
        out_shape=jax.ShapeDtypeStruct(potential.shape, f32),
        in_specs=[far, far, pl.BlockSpec(memory_space=pltpu.SMEM), far, far, far, far],
        out_specs=vm,
        scratch_shapes=[
            pltpu.VMEM((slices, W, W), f32),
            pltpu.VMEM((6, W, W), f32),
            pltpu.VMEM((2, W, W), f32),
            pltpu.VMEM((3, W, W), f32),
            pltpu.VMEM((slices, 2, W, W), f32),
            pltpu.VMEM((2 * layers, 2, W, W), f32),
            pltpu.VMEM((2, W, W), f32),
            pltpu.VMEM((2, 8, 128), jnp.int32),
            pltpu.VMEM((2, 2, 8, 128), jnp.int32),
            pltpu.VMEM((2, layers, strip, W), f32),
            pltpu.VMEM((2, layers, strip, W), f32),
            pltpu.VMEM((2, 2 * layers, strip, W), f32),
            pltpu.VMEM((2 * layers, strip, W), f32),
            pltpu.VMEM((2, layers, strip, W), f32),
            pltpu.VMEM((layers, strip, W), f32),
            pltpu.VMEM((3, columns, W), bf16),
            dma((2,)), dma((2,)), dma((2, layers)), dma((2, layers)),
            dma((layers, 2)), dma((slices,)), dma((6, 3)), dma((6,)),
            dma((2, 2 * layers)), dma((2, layers)), dma((layers,)), dma((layers,)),
            dma((3,)), dma((2,)),
            pltpu.VMEM(potential.shape, f32),
            pltpu.VMEM(probe.shape, f32),
            pltpu.VMEM(intensity.shape, f32),
            pltpu.VMEM(T.shape, bf16),
            pltpu.VMEM(Fr.shape, bf16),
            pltpu.VMEM(phase.shape, f32),
            dma((6,)),
        ],
        compiler_params=pltpu.CompilerParams(
            collective_id=0, has_side_effects=True, vmem_limit_bytes=56 << 20
        ),
    )(potential, probe, positions, intensity, jnp.asarray(T), jnp.asarray(Fr), jnp.asarray(phase))


def solution(mesh):
    in_specs = (P("depth", "probe", None), P(), P("probe", None), P("probe", None, None))
    out_specs = P("depth", "probe", None)
    return jax.shard_map(local, mesh=mesh, in_specs=in_specs, out_specs=out_specs, check_vma=False)
```

```python
import functools

import jax
import jax.numpy as jnp
import ml_dtypes
import numpy as np
from jax import lax
from jax.experimental import pallas as pl
from jax.experimental.pallas import tpu as pltpu
from jax.sharding import PartitionSpec as P
W=256; HB=128
f32=jnp.float32; bf16=jnp.bfloat16

def fit(fn, degree, top):
    n=64
    z=(np.cos(np.pi*(np.arange(n)+.5)/n)+1)*top/2
    return np.polynomial.chebyshev.Chebyshev.fit(z, fn(z), degree, domain=[0,top]).convert(kind=np.polynomial.Polynomial).coef
SINC=fit(lambda z: np.sin(np.sqrt(z))/np.sqrt(z),6,9.0)
COSC=fit(lambda z: np.cos(np.sqrt(z)),6,9.0)

def halves(a):
    hi=a.astype(np.float32).astype(ml_dtypes.bfloat16)
    lo=(a-hi.astype(np.float64)).astype(np.float32).astype(ml_dtypes.bfloat16)
    return hi,lo

def tables():
    k=np.arange(W)
    F=np.exp(-2j*np.pi*((k[:,None]*k[None,:])%W)/W)/np.sqrt(W)
    fr=(((k+W//2)%W)-W//2)/W
    h=np.exp(-60j*fr*fr)
    A=np.conj(F)@np.diag(h)@F
    order=np.concatenate([np.arange(HB), W-1-np.arange(HB)])
    PP=A[:HB,:HB]; Q=A[:HB][:,order[HB:]]
    out=[]
    for B in ((PP+Q)/2,(PP-Q)/2):
        right=np.block([[B.real,B.imag],[-B.imag,B.real]])
        left=np.block([[B.real,-B.imag],[B.imag,B.real]])
        out.append((right,left))
    prop=[out[0][0],out[1][0],out[0][1],out[1][1]]
    half=np.arange(HB)+.5
    turn=2*np.pi/W*half[:,None]*half[None,:]
    zero=np.zeros((HB,HB))
    waves=np.block([[np.cos(turn),zero],[zero,np.sin(turn)]])/np.sqrt(W)
    shift=np.exp(2j*np.pi*(order/(2*W)+1/(8*W)))
    phase=shift[:,None]*shift[None,:]
    hp,lp=zip(*[halves(a) for a in prop])
    return (np.stack([np.stack(hp),np.stack(lp)]), np.stack(halves(waves)),
            np.stack([phase.real,phase.imag]).astype(np.float32))

def split(x):
    hi=x.astype(bf16)
    return hi,(x-hi.astype(f32)).astype(bf16)

def dot(a,b):
    return lax.dot_general(a,b,(((1,),(0,)),((),())),preferred_element_type=f32)

def mm_right(x, wh, wl):
    h,l=split(x)
    y=dot(jnp.concatenate([h,l],0),wh)
    return y[:W]+y[W:]+dot(h,wl)
def mm_left(wh,wl,x):
    h,l=split(x)
    y=dot(jnp.concatenate([wh,wl],0),h)
    return y[:W]+y[W:]+dot(wh,l)

def propagate(ur,ui,T):
    ure,uro=ur[:,:HB]+ur[:,HB:],ur[:,:HB]-ur[:,HB:]
    uie,uio=ui[:,:HB]+ui[:,HB:],ui[:,:HB]-ui[:,HB:]
    ye=mm_right(jnp.concatenate([ure,uie],1),T[0,0],T[1,0])
    yo=mm_right(jnp.concatenate([uro,uio],1),T[0,1],T[1,1])
    te,be=ye[:HB]+ye[HB:],ye[:HB]-ye[HB:]
    to,bo=yo[:HB]+yo[HB:],yo[:HB]-yo[HB:]
    re=jnp.concatenate([jnp.concatenate([te[:,:HB],to[:,:HB]],1),jnp.concatenate([te[:,HB:],to[:,HB:]],1)],0)
    ro=jnp.concatenate([jnp.concatenate([be[:,:HB],bo[:,:HB]],1),jnp.concatenate([be[:,HB:],bo[:,HB:]],1)],0)
    ze=mm_left(T[0,2],T[1,2],re)
    zo=mm_left(T[0,3],T[1,3],ro)
    top=ze+zo; bot=ze-zo
    def unfold(t,b):
        return jnp.concatenate([jnp.concatenate([t[:,:HB]+t[:,HB:],t[:,:HB]-t[:,HB:]],1),
                                jnp.concatenate([b[:,:HB]+b[:,HB:],b[:,:HB]-b[:,HB:]],1)],0)
    return unfold(top[:HB],bot[:HB]),unfold(top[HB:],bot[HB:])

def shifted_right(xr,xi,w):
    def parts(x):
        p=mm_right(jnp.concatenate([x[:,:HB]-x[:,HB:],x[:,:HB]+x[:,HB:]],1),w[0],w[1])
        return p[:,:HB],p[:,HB:]
    (ar,br),(ai,bi)=parts(xr),parts(xi)
    return jnp.concatenate([bi+ar,bi-ar],1),jnp.concatenate([ai-br,-ai-br],1)

def shifted_left(w,xr,xi):
    def parts(x):
        p=mm_left(w[0],w[1],jnp.concatenate([x[:HB]-x[HB:],x[:HB]+x[HB:]],0))
        return p[:HB],p[HB:]
    (ar,br),(ai,bi)=parts(xr),parts(xi)
    return jnp.concatenate([bi+ar,bi-ar],0),jnp.concatenate([ai-br,-ai-br],0)

def poly(c,z):
    r=jnp.full_like(z,float(c[-1]))
    for a in c[-2::-1]:
        r=r*z+float(a)
    return r
def sincos(v):
    x=0.5*v; z=x*x
    return poly(COSC,z), x*poly(SINC,z)

def detector(ur,ui,inten,Fr,phase):
    er,ei=phase[0],phase[1]
    yr,yi=shifted_right(er*ur-ei*ui,er*ui+ei*ur,Fr)
    vr,vi=shifted_left(Fr,yr,yi)
    m=vr*vr+vi*vi-inten
    yr,yi=shifted_right(m*vr,-(m*vi),Fr)
    zr,zi=shifted_left(Fr,yr,yi)
    return er*zr-ei*zi,er*zi+ei*zr

def select_right(x, chosen):
    high, low = split(x)
    return dot(high, chosen) + dot(low, chosen)


def select_left(chosen, x):
    high, low = split(x)
    return dot(chosen, high) + dot(chosen, low)


def spread(x, chosen):
    return sum(
        lax.dot_general(part, chosen, (((1,), (1,)), ((), ())), preferred_element_type=f32)
        for part in split(x)
    )


def folded(shape, dim):
    index = lax.broadcasted_iota(jnp.int32, shape, dim)
    return jnp.where(index < HB, index, W + HB - 1 - index)


def ones_where(condition):
    return jnp.where(condition, 1.0, 0.0).astype(bf16)


def wide(row, width):
    return jnp.concatenate([row] * (width // 128), axis=1)


def kernel(
    groups, depths, v_hbm, p_hbm, pos_ref, i_hbm, T_hbm, Fr_hbm, phase_hbm, o_ref,
    V, held, wave_in, wave_out, cs, us, ps, pos_out, pos_in, halo_out, halo_in, dep_out, dep_mid, dep_in, own_cut, pick,
    pos_ss, pos_rs, halo_ss, halo_rs, send_v, recv_v, held_s, held_r, dep_ss, dep_rs, mid_s, mid_r, wave_s, wave_r, v_ref, p_ref, i_ref, T, Fr, phase, load_s,
):
    layers, strip, columns = v_hbm.shape
    slices = layers * depths
    rows = groups * strip
    g = lax.axis_index("probe")
    d = lax.axis_index("depth")
    y = d // 2
    xl = d % 2
    core = g % 2
    active = xl == core
    before, after = (g + groups - 1) % groups, (g + 1) % groups
    beside = g + 1 - 2 * core
    partner = d + 1 - 2 * xl
    up, down = (d + 2) % depths, (d + depths - 2) % depths

    def there(probe_at, depth_at):
        return {"probe": probe_at, "depth": depth_at}

    barrier = pltpu.get_barrier_semaphore()
    peers = [there(near_by, at) for near_by in (before, after) for at in (d, partner)]
    peers += [there(g, partner)]
    peers += [there(near_by, at) for near_by in (g, beside) for at in (up, down)]
    across = (d + depths // 2) % depths
    peers += [there(g, across)]
    for peer in peers:
        pl.semaphore_signal(barrier, inc=1, device_id=peer, device_id_type=pl.DeviceIdType.MESH)
    loads = [
        pltpu.make_async_copy(source, target, load_s.at[k])
        for k, (source, target) in enumerate(
            [(v_hbm, v_ref), (p_hbm, p_ref), (i_hbm, i_ref), (T_hbm, T), (Fr_hbm, Fr), (phase_hbm, phase)]
        )
    ]
    for load in loads:
        load.start()
    pos_out[0] = jnp.full((8, 128), pos_ref[0, 0], jnp.int32)
    pos_out[1] = jnp.full((8, 128), pos_ref[0, 1], jnp.int32)
    pl.semaphore_wait(barrier, len(peers))

    def remote(source, target, sent, received, where):
        return pltpu.make_async_remote_copy(
            src_ref=source, dst_ref=target, send_sem=sent, recv_sem=received,
            device_id=where, device_id_type=pl.DeviceIdType.MESH,
        )

    near = (there(before, d), there(after, d))
    pos_copy = [remote(pos_out, pos_in.at[1 - n], pos_ss.at[n], pos_rs.at[1 - n], near[n]) for n in (0, 1)]
    for n in (0, 1):
        pos_copy[n].start()

    lines = lax.broadcasted_iota(jnp.int32, (columns, W), 0)
    place = folded((columns, W), 1)

    def column_pick(left):
        return ones_where(lines == place + wide(left, W))

    pick[2] = column_pick(pos_out[1][:1])
    for load in loads:
        load.wait()
    for s in range(layers):
        own_cut[s] = select_right(v_ref[s], pick[2])
    fold = ones_where(lax.broadcasted_iota(jnp.int32, (W, W), 0) == folded((W, W), 1))
    for c in (0, 1):
        ps[c] = select_left(fold, select_right(p_ref[c], fold))
    i_ref[0] = select_left(fold, select_right(i_ref[0], fold))
    offset = (pos_out[0][:1] - (g - 1) * strip + rows) & (rows - 1)
    row_pick = ones_where(
        lax.broadcasted_iota(jnp.int32, (W, 3 * strip), 1) == folded((W, 3 * strip), 0) + wide(offset, 3 * strip)
    )
    row_back = ones_where(
        lax.broadcasted_iota(jnp.int32, (3 * strip, W), 0) == folded((3 * strip, W), 1) + wide(offset, W)
    )

    halo_copy = [
        [remote(halo_out.at[n, s], halo_in.at[1 - n, s], halo_ss.at[n, s], halo_rs.at[1 - n, s], near[n]) for s in range(layers)]
        for n in (0, 1)
    ]
    near_first = (1 - core, core)
    for n in near_first:
        remote(pos_out, pos_in.at[n], pos_ss.at[n], pos_rs.at[n], near[0]).wait_recv()
        pick[n] = column_pick(pos_in[n, 1][:1])
        to = there(jnp.where(n == 0, before, after), d)
        for s in range(layers):
            halo_out[n, s] = select_right(v_ref[s], pick[n])
            remote(halo_out.at[n, s], halo_in.at[1 - n, s], halo_ss.at[n, s], halo_rs.at[1 - n, s], to).start()

    def into_window(source, slice_at, sent, probe_at, depth_at):
        return remote(source, V.at[slice_at], sent, recv_v.at[slice_at], there(probe_at, depth_at))

    def into_held(source, k, sent, probe_at, depth_at):
        return remote(source, held.at[k], sent, held_r.at[k], there(probe_at, depth_at))

    def needs(target, group):
        target, group = (target + 4) % 4, (group + 4) % 4
        return (target < 2) | ((target == 2) & (group == 3))

    def own_sends(s):
        mine = layers * d + s
        if s == 0:
            return (
                (needs(y + 2, y), into_held(V.at[mine], 2, send_v.at[s, 0], beside, up)),
                (needs(y + 1, y) & ~needs(y + 2, y), into_window(V.at[mine], mine, send_v.at[s, 0], g, up)),
                (needs(y - 1, y), into_window(V.at[mine], mine, send_v.at[s, 1], g, down)),
            )
        return (
            (needs(y - 2, y), into_held(V.at[mine], 4, send_v.at[s, 1], beside, down)),
            (needs(y - 1, y) & ~needs(y - 2, y), into_window(V.at[mine], mine, send_v.at[s, 1], g, down)),
            (needs(y + 1, y), into_window(V.at[mine], mine, send_v.at[s, 0], g, up)),
        )

    def other_send(s):
        return into_held(V.at[layers * d + s], s, send_v.at[s, 0], beside, partner)

    def start_each(pairs):
        for condition, copy in pairs:
            pl.when(condition)(copy.start)

    def end_each(pairs):
        for condition, copy in pairs:
            pl.when(condition)(copy.wait_send)

    for s in range(layers):
        mine = layers * d + s
        halo_copy[1][s].wait_recv()
        halo_copy[0][s].wait_recv()
        tall = jnp.concatenate([halo_in[0, s], own_cut[s], halo_in[1, s]], axis=0)
        V[mine] = select_left(row_pick, tall)

        @pl.when(active)
        def _():
            copies = own_sends(s)
            if s == 0:
                start_each(copies[:2])
                pl.when(copies[2][0] & (y != 2))(copies[2][1].start)
            else:
                start_each(copies)

                @pl.when(y == 2)
                def _():
                    copies[0][1].wait_send()
                    own_sends(0)[2][1].start()

        @pl.when(jnp.logical_not(active))
        def _():
            other_send(s).start()

    per = 2 * layers

    def passing():
        low, high = (partner + depths - 2) % depths, (partner + 2) % depths

        always = y >= 0

        def home(k, slice_at, condition):
            return condition, into_window(held.at[k], slice_at, held_s.at[k, 0], beside, d)

        def window(k, slice_at, condition, where):
            return condition, into_window(held.at[k], slice_at, held_s.at[k, 1], beside, where)

        def direct(k, slice_at, condition, where):
            return condition, into_window(held.at[k], slice_at, held_s.at[k, 2], beside, where)

        def onward(k, to, condition, where):
            return condition, into_held(held.at[k], to, held_s.at[k, 2], g, where)

        first, second = layers * partner, layers * partner + 1
        to_up, to_down = needs(y + 1, y - 1), needs(y - 1, y + 1)
        here_low, here_high = needs(y, y - 1), needs(y, y + 1)
        own_low, own_high = layers * down, layers * up + 1
        part_low, part_high = layers * low, layers * high + 1
        return (
            (0, always, (
                onward(0, 3, needs(y + 2, y), up), direct(0, first, needs(y + 1, y) & ~needs(y + 2, y), up),
                window(0, first, needs(y - 1, y), down), home(0, first, always))),
            (1, always, (
                onward(1, 5, needs(y - 2, y), down), direct(1, second, needs(y - 1, y) & ~needs(y - 2, y), down),
                window(1, second, needs(y + 1, y), up), home(1, second, always))),
            (2, to_up, (window(2, own_low, to_up, up), home(2, own_low, to_up & here_low))),
            (4, to_down, (window(4, own_high, to_down, down), home(4, own_high, to_down & here_high))),
            (3, to_up, (window(3, part_low, to_up, up), home(3, part_low, to_up & here_low))),
            (5, to_down, (window(5, part_high, to_down, down), home(5, part_high, to_down & here_high))),
        )

    @pl.when(jnp.logical_not(active))
    def _():
        for k, comes, copies in passing():
            @pl.when(comes)
            def _():
                into_held(held.at[k], k, held_s.at[k, 0], beside, d).wait_recv()
                if k == 0:
                    pl.when(copies[2][0] & (y != 2))(copies[2][1].start)
                    pl.when(copies[0][0] & (y != 3))(copies[0][1].start)
                    start_each(copies[1:2] + copies[3:])
                elif k == 1:
                    pl.when(copies[2][0] & (y != 3))(copies[2][1].start)
                    start_each(copies[:2] + copies[3:])
                else:
                    start_each(copies)

                if k == 3:
                    @pl.when(y == 3)
                    def _():
                        copies[0][1].wait_send()
                        passing()[0][2][0][1].start()
                        passing()[1][2][2][1].start()

            if k == 1:
                @pl.when(y == 2)
                def _():
                    copies[0][1].wait_send()
                    passing()[0][2][2][1].start()

    def edge_copy(n, slot):
        return remote(
            dep_out.at[n, slot], dep_in.at[1 - n, slot % layers], dep_ss.at[n, slot],
            dep_rs.at[1 - n, slot % layers], there((before, after)[n], 2 * y + slot // layers),
        )

    def middle_copy(slot):
        return remote(dep_mid.at[slot], dep_mid.at[slot], mid_s.at[slot % layers], mid_r.at[slot % layers], there(g, partner))

    def trans(s, ar, ai):
        c, n = cs[s, 0], cs[s, 1]
        return c * ar - n * ai, c * ai + n * ar

    @pl.when(active)
    def _():
        def arrive(s):
            @pl.when(s // layers != d)
            def _():
                into_window(V.at[s], s, send_v.at[0, 0], g, partner).wait_recv()

        def prepare(s):
            arrive(s)
            c, n = sincos(V[s])
            cs[s, 0] = c
            cs[s, 1] = n

        ready = jnp.where(y == 0, layers * core, per * y)
        ready_end = jnp.where(y == 0, 2 * layers * core, jnp.where(y == 2, slices, per * (y + 1)))

        def wave_copy(k, to, where):
            return remote(wave_out.at[k], wave_in.at[to], wave_s.at[k], wave_r.at[to], there(g, where))

        @pl.loop(ready, ready_end)
        def _(s):
            prepare(s)

        @pl.when(y >= 2)
        def _():
            for c in (0, 1):
                wave_copy(c, c, down).wait_recv()
                ps[c] = wave_in[c]

        def enter(s):
            @pl.when((s < ready) | (s >= ready_end))
            def _():
                prepare(s)

            c, n = cs[s, 0], cs[s, 1]
            ar, ai = ps[0], ps[1]
            ur, ui = c * ar - n * ai, c * ai + n * ar

            @pl.when(s // per == y)
            def _():
                us[s % per, 0] = ur
                us[s % per, 1] = ui

            return ur, ui

        def leave(s, qr, qi):
            @pl.when(s // per == y)
            def _():
                slot = s % per
                tall = select_left(row_back, -0.5 * (qr * us[slot, 1] + qi * us[slot, 0]))
                dep_out[0, slot] = tall[:strip]
                edge_copy(0, slot).start()
                dep_out[1, slot] = tall[2 * strip :]
                edge_copy(1, slot).start()
                dep_mid[slot] = tall[strip : 2 * strip]

                @pl.when(slot // layers != xl)
                def _():
                    middle_copy(slot).start()

        @pl.loop(jnp.where(y < 2, 0, per * y), slices - 1)
        def _(s):
            ur, ui = enter(s)
            ps[0], ps[1] = propagate(ur, ui, T)

            @pl.when((y == 1) & (s == 2 * per - 1))
            def _():
                wave_out[0] = ps[0]
                wave_copy(0, 0, up).start()

            @pl.when((y == 0) & (s == 2 * per - 1))
            def _():
                wave_out[0] = ps[1]
                wave_copy(0, 1, across).start()

            @pl.when((y == 0) & (s == 3 * per - 1))
            def _():
                for c in (0, 1):
                    wave_out[1 + c] = ps[c]
                    wave_copy(1 + c, c, down).start()

        ur, ui = enter(slices - 1)
        qr, qi = detector(ur, ui, i_ref[0], Fr, phase)

        @pl.when(y < 2)
        def _():
            wave_copy(0, 0, up).wait_send()

        @pl.when(y == 0)
        def _():
            for c in (0, 1):
                wave_copy(1 + c, c, down).wait_send()

        ps[0] = qr
        ps[1] = qi
        leave(slices - 1, qr, qi)

        @pl.loop(0, slices - 1 - per * y)
        def _(t):
            s = slices - 2 - t
            gr, gi = trans(s + 1, ps[0], ps[1])
            qr, qi = propagate(gr, gi, T)
            ps[0] = qr
            ps[1] = qi
            leave(s, qr, qi)

    for s in (1, 0):
        slot = layers * xl + s

        @pl.when(jnp.logical_not(active))
        def _():
            middle_copy(slot).wait_recv()

        total = spread(dep_mid[slot], pick[2])
        for n in near_first:
            remote(dep_out.at[n, slot], dep_in.at[n, s], dep_ss.at[n, slot], dep_rs.at[n, s], near[0]).wait_recv()
            total += spread(dep_in[n, s], pick[n])
        o_ref[s] = total

    for n in (0, 1):
        pos_copy[n].wait_send()
        for s in range(layers):
            halo_copy[n][s].wait_send()

    @pl.when(jnp.logical_not(active))
    def _():
        for s in range(layers):
            other_send(s).wait_send()
        for k, comes, copies in passing():
            if k == 1:
                end_each(copies[1:])
                pl.when(copies[0][0] & (y != 2))(copies[0][1].wait_send)
            elif k == 3:
                end_each(copies[1:])
                pl.when(copies[0][0] & (y != 3))(copies[0][1].wait_send)
            else:
                end_each(copies)

    @pl.when(active)
    def _():
        for s in range(layers):
            copies = own_sends(s)
            if s == 0:
                end_each(copies)
            else:
                end_each(copies[1:])
                pl.when(copies[0][0] & (y != 2))(copies[0][1].wait_send)
            middle_copy(layers * (1 - xl) + s).wait_send()
        for slot in range(per):
            for n in (0, 1):
                edge_copy(n, slot).wait_send()


def local(potential, probe, positions, intensity):
    layers, strip, columns = potential.shape
    groups = lax.axis_size("probe")
    depths = lax.axis_size("depth")
    slices = layers * depths
    T, Fr, phase = tables()
    vm = pl.BlockSpec(memory_space=pltpu.VMEM)
    far = pl.BlockSpec(memory_space=pl.ANY)
    dma = pltpu.SemaphoreType.DMA
    return pl.pallas_call(
        functools.partial(kernel, groups, depths),
        out_shape=jax.ShapeDtypeStruct(potential.shape, f32),
        in_specs=[far, far, pl.BlockSpec(memory_space=pltpu.SMEM), far, far, far, far],
        out_specs=vm,
        scratch_shapes=[
            pltpu.VMEM((slices, W, W), f32),
            pltpu.VMEM((6, W, W), f32),
            pltpu.VMEM((2, W, W), f32),
            pltpu.VMEM((3, W, W), f32),
            pltpu.VMEM((slices, 2, W, W), f32),
            pltpu.VMEM((2 * layers, 2, W, W), f32),
            pltpu.VMEM((2, W, W), f32),
            pltpu.VMEM((2, 8, 128), jnp.int32),
            pltpu.VMEM((2, 2, 8, 128), jnp.int32),
            pltpu.VMEM((2, layers, strip, W), f32),
            pltpu.VMEM((2, layers, strip, W), f32),
            pltpu.VMEM((2, 2 * layers, strip, W), f32),
            pltpu.VMEM((2 * layers, strip, W), f32),
            pltpu.VMEM((2, layers, strip, W), f32),
            pltpu.VMEM((layers, strip, W), f32),
            pltpu.VMEM((3, columns, W), bf16),
            dma((2,)), dma((2,)), dma((2, layers)), dma((2, layers)),
            dma((layers, 2)), dma((slices,)), dma((6, 3)), dma((6,)),
            dma((2, 2 * layers)), dma((2, layers)), dma((layers,)), dma((layers,)),
            dma((3,)), dma((2,)),
            pltpu.VMEM(potential.shape, f32),
            pltpu.VMEM(probe.shape, f32),
            pltpu.VMEM(intensity.shape, f32),
            pltpu.VMEM(T.shape, bf16),
            pltpu.VMEM(Fr.shape, bf16),
            pltpu.VMEM(phase.shape, f32),
            dma((6,)),
        ],
        compiler_params=pltpu.CompilerParams(
            collective_id=0, has_side_effects=True, vmem_limit_bytes=56 << 20
        ),
    )(potential, probe, positions, intensity, jnp.asarray(T), jnp.asarray(Fr), jnp.asarray(phase))


def solution(mesh):
    in_specs = (P("depth", "probe", None), P(), P("probe", None), P("probe", None, None))
    out_specs = P("depth", "probe", None)
    return jax.shard_map(local, mesh=mesh, in_specs=in_specs, out_specs=out_specs, check_vma=False)
```

```python
import functools

import jax
import jax.numpy as jnp
import ml_dtypes
import numpy as np
from jax import lax
from jax.experimental import pallas as pl
from jax.experimental.pallas import tpu as pltpu
from jax.sharding import PartitionSpec as P
W=256; HB=128
f32=jnp.float32; bf16=jnp.bfloat16

def fit(fn, degree, top):
    n=64
    z=(np.cos(np.pi*(np.arange(n)+.5)/n)+1)*top/2
    return np.polynomial.chebyshev.Chebyshev.fit(z, fn(z), degree, domain=[0,top]).convert(kind=np.polynomial.Polynomial).coef
SINC=fit(lambda z: np.sin(np.sqrt(z))/np.sqrt(z),6,9.0)
COSC=fit(lambda z: np.cos(np.sqrt(z)),6,9.0)

def halves(a):
    hi=a.astype(np.float32).astype(ml_dtypes.bfloat16)
    lo=(a-hi.astype(np.float64)).astype(np.float32).astype(ml_dtypes.bfloat16)
    return hi,lo

def tables():
    k=np.arange(W)
    F=np.exp(-2j*np.pi*((k[:,None]*k[None,:])%W)/W)/np.sqrt(W)
    fr=(((k+W//2)%W)-W//2)/W
    h=np.exp(-60j*fr*fr)
    A=np.conj(F)@np.diag(h)@F
    order=np.concatenate([np.arange(HB), W-1-np.arange(HB)])
    PP=A[:HB,:HB]; Q=A[:HB][:,order[HB:]]
    out=[]
    for B in ((PP+Q)/2,(PP-Q)/2):
        right=np.block([[B.real,B.imag],[-B.imag,B.real]])
        left=np.block([[B.real,-B.imag],[B.imag,B.real]])
        out.append((right,left))
    prop=[out[0][0],out[1][0],out[0][1],out[1][1]]
    half=np.arange(HB)+.5
    turn=2*np.pi/W*half[:,None]*half[None,:]
    zero=np.zeros((HB,HB))
    waves=np.block([[np.cos(turn),zero],[zero,np.sin(turn)]])/np.sqrt(W)
    shift=np.exp(2j*np.pi*(order/(2*W)+1/(8*W)))
    phase=shift[:,None]*shift[None,:]
    hp,lp=zip(*[halves(a) for a in prop])
    return (np.stack([np.stack(hp),np.stack(lp)]), np.stack(halves(waves)),
            np.stack([phase.real,phase.imag]).astype(np.float32))

def split(x):
    hi=x.astype(bf16)
    return hi,(x-hi.astype(f32)).astype(bf16)

def dot(a,b):
    return lax.dot_general(a,b,(((1,),(0,)),((),())),preferred_element_type=f32)

def mm_right(x, wh, wl):
    h,l=split(x)
    y=dot(jnp.concatenate([h,l],0),wh)
    return y[:W]+y[W:]+dot(h,wl)
def mm_left(wh,wl,x):
    h,l=split(x)
    y=dot(jnp.concatenate([wh,wl],0),h)
    return y[:W]+y[W:]+dot(wh,l)

def propagate(ur,ui,T):
    ure,uro=ur[:,:HB]+ur[:,HB:],ur[:,:HB]-ur[:,HB:]
    uie,uio=ui[:,:HB]+ui[:,HB:],ui[:,:HB]-ui[:,HB:]
    ye=mm_right(jnp.concatenate([ure,uie],1),T[0,0],T[1,0])
    yo=mm_right(jnp.concatenate([uro,uio],1),T[0,1],T[1,1])
    te,be=ye[:HB]+ye[HB:],ye[:HB]-ye[HB:]
    to,bo=yo[:HB]+yo[HB:],yo[:HB]-yo[HB:]
    re=jnp.concatenate([jnp.concatenate([te[:,:HB],to[:,:HB]],1),jnp.concatenate([te[:,HB:],to[:,HB:]],1)],0)
    ro=jnp.concatenate([jnp.concatenate([be[:,:HB],bo[:,:HB]],1),jnp.concatenate([be[:,HB:],bo[:,HB:]],1)],0)
    ze=mm_left(T[0,2],T[1,2],re)
    zo=mm_left(T[0,3],T[1,3],ro)
    top=ze+zo; bot=ze-zo
    def unfold(t,b):
        return jnp.concatenate([jnp.concatenate([t[:,:HB]+t[:,HB:],t[:,:HB]-t[:,HB:]],1),
                                jnp.concatenate([b[:,:HB]+b[:,HB:],b[:,:HB]-b[:,HB:]],1)],0)
    return unfold(top[:HB],bot[:HB]),unfold(top[HB:],bot[HB:])

def shifted_right(xr,xi,w):
    def parts(x):
        p=mm_right(jnp.concatenate([x[:,:HB]-x[:,HB:],x[:,:HB]+x[:,HB:]],1),w[0],w[1])
        return p[:,:HB],p[:,HB:]
    (ar,br),(ai,bi)=parts(xr),parts(xi)
    return jnp.concatenate([bi+ar,bi-ar],1),jnp.concatenate([ai-br,-ai-br],1)

def shifted_left(w,xr,xi):
    def parts(x):
        p=mm_left(w[0],w[1],jnp.concatenate([x[:HB]-x[HB:],x[:HB]+x[HB:]],0))
        return p[:HB],p[HB:]
    (ar,br),(ai,bi)=parts(xr),parts(xi)
    return jnp.concatenate([bi+ar,bi-ar],0),jnp.concatenate([ai-br,-ai-br],0)

def poly(c,z):
    r=jnp.full_like(z,float(c[-1]))
    for a in c[-2::-1]:
        r=r*z+float(a)
    return r
def sincos(v):
    x=0.5*v; z=x*x
    return poly(COSC,z), x*poly(SINC,z)

def detector(ur,ui,inten,Fr,phase):
    er,ei=phase[0],phase[1]
    yr,yi=shifted_right(er*ur-ei*ui,er*ui+ei*ur,Fr)
    vr,vi=shifted_left(Fr,yr,yi)
    m=vr*vr+vi*vi-inten
    yr,yi=shifted_right(m*vr,-(m*vi),Fr)
    zr,zi=shifted_left(Fr,yr,yi)
    return er*zr-ei*zi,er*zi+ei*zr

def select_right(x, chosen):
    high, low = split(x)
    return dot(high, chosen) + dot(low, chosen)


def select_left(chosen, x):
    high, low = split(x)
    return dot(chosen, high) + dot(chosen, low)


def spread(x, chosen):
    return sum(
        lax.dot_general(part, chosen, (((1,), (1,)), ((), ())), preferred_element_type=f32)
        for part in split(x)
    )


def folded(shape, dim):
    index = lax.broadcasted_iota(jnp.int32, shape, dim)
    return jnp.where(index < HB, index, W + HB - 1 - index)


def ones_where(condition):
    return jnp.where(condition, 1.0, 0.0).astype(bf16)


def wide(row, width):
    return jnp.concatenate([row] * (width // 128), axis=1)


def kernel(
    groups, depths, v_hbm, p_hbm, pos_ref, i_hbm, T_hbm, Fr_hbm, phase_hbm, o_ref,
    V, held, wave_in, wave_out, cs, us, ps, pos_out, pos_in, halo_out, halo_in, dep_out, dep_mid, dep_in, own_cut, pick,
    pos_ss, pos_rs, halo_ss, halo_rs, send_v, recv_v, held_s, held_r, dep_ss, dep_rs, mid_s, mid_r, wave_s, wave_r, v_ref, p_ref, i_ref, T, Fr, phase, load_s,
):
    layers, strip, columns = v_hbm.shape
    slices = layers * depths
    rows = groups * strip
    g = lax.axis_index("probe")
    d = lax.axis_index("depth")
    y = d // 2
    xl = d % 2
    core = g % 2
    active = xl == core
    before, after = (g + groups - 1) % groups, (g + 1) % groups
    beside = g + 1 - 2 * core
    partner = d + 1 - 2 * xl
    up, down = (d + 2) % depths, (d + depths - 2) % depths

    def there(probe_at, depth_at):
        return {"probe": probe_at, "depth": depth_at}

    barrier = pltpu.get_barrier_semaphore()
    peers = [there(near_by, at) for near_by in (before, after) for at in (d, partner)]
    peers += [there(g, partner)]
    peers += [there(near_by, at) for near_by in (g, beside) for at in (up, down)]
    across = (d + depths // 2) % depths
    peers += [there(g, across)]
    for peer in peers:
        pl.semaphore_signal(barrier, inc=1, device_id=peer, device_id_type=pl.DeviceIdType.MESH)
    loads = [
        pltpu.make_async_copy(source, target, load_s.at[k])
        for k, (source, target) in enumerate(
            [(v_hbm, v_ref), (p_hbm, p_ref), (i_hbm, i_ref), (T_hbm, T), (Fr_hbm, Fr), (phase_hbm, phase)]
        )
    ]
    for load in loads:
        load.start()
    pos_out[0] = jnp.full((8, 128), pos_ref[0, 0], jnp.int32)
    pos_out[1] = jnp.full((8, 128), pos_ref[0, 1], jnp.int32)
    pl.semaphore_wait(barrier, len(peers))

    def remote(source, target, sent, received, where):
        return pltpu.make_async_remote_copy(
            src_ref=source, dst_ref=target, send_sem=sent, recv_sem=received,
            device_id=where, device_id_type=pl.DeviceIdType.MESH,
        )

    near = (there(before, d), there(after, d))
    pos_copy = [remote(pos_out, pos_in.at[1 - n], pos_ss.at[n], pos_rs.at[1 - n], near[n]) for n in (0, 1)]
    for n in (0, 1):
        pos_copy[n].start()

    lines = lax.broadcasted_iota(jnp.int32, (columns, W), 0)
    place = folded((columns, W), 1)

    def column_pick(left):
        return ones_where(lines == place + wide(left, W))

    pick[2] = column_pick(pos_out[1][:1])
    for load in loads:
        load.wait()
    for s in range(layers):
        own_cut[s] = select_right(v_ref[s], pick[2])
    fold = ones_where(lax.broadcasted_iota(jnp.int32, (W, W), 0) == folded((W, W), 1))
    for c in (0, 1):
        ps[c] = select_left(fold, select_right(p_ref[c], fold))
    i_ref[0] = select_left(fold, select_right(i_ref[0], fold))
    offset = (pos_out[0][:1] - (g - 1) * strip + rows) & (rows - 1)
    row_pick = ones_where(
        lax.broadcasted_iota(jnp.int32, (W, 3 * strip), 1) == folded((W, 3 * strip), 0) + wide(offset, 3 * strip)
    )
    row_back = ones_where(
        lax.broadcasted_iota(jnp.int32, (3 * strip, W), 0) == folded((3 * strip, W), 1) + wide(offset, W)
    )

    halo_copy = [
        [remote(halo_out.at[n, s], halo_in.at[1 - n, s], halo_ss.at[n, s], halo_rs.at[1 - n, s], near[n]) for s in range(layers)]
        for n in (0, 1)
    ]
    near_first = (1 - core, core)
    for n in near_first:
        remote(pos_out, pos_in.at[n], pos_ss.at[n], pos_rs.at[n], near[0]).wait_recv()
        pick[n] = column_pick(pos_in[n, 1][:1])
        to = there(jnp.where(n == 0, before, after), d)
        for s in range(layers):
            halo_out[n, s] = select_right(v_ref[s], pick[n])
            remote(halo_out.at[n, s], halo_in.at[1 - n, s], halo_ss.at[n, s], halo_rs.at[1 - n, s], to).start()

    def into_window(source, slice_at, sent, probe_at, depth_at):
        return remote(source, V.at[slice_at], sent, recv_v.at[slice_at], there(probe_at, depth_at))

    def into_held(source, k, sent, probe_at, depth_at):
        return remote(source, held.at[k], sent, held_r.at[k], there(probe_at, depth_at))

    def needs(target, group):
        target, group = (target + 4) % 4, (group + 4) % 4
        return (target < 2) | ((target == 2) & (group == 3))

    def own_sends(s):
        mine = layers * d + s
        if s == 0:
            return (
                (needs(y + 2, y), into_held(V.at[mine], 2, send_v.at[s, 0], beside, up)),
                (needs(y + 1, y) & ~needs(y + 2, y), into_window(V.at[mine], mine, send_v.at[s, 0], g, up)),
                (needs(y - 1, y), into_window(V.at[mine], mine, send_v.at[s, 1], g, down)),
            )
        return (
            (needs(y - 2, y), into_held(V.at[mine], 4, send_v.at[s, 1], beside, down)),
            (needs(y - 1, y) & ~needs(y - 2, y), into_window(V.at[mine], mine, send_v.at[s, 1], g, down)),
            (needs(y + 1, y), into_window(V.at[mine], mine, send_v.at[s, 0], g, up)),
        )

    def other_send(s):
        return into_held(V.at[layers * d + s], s, send_v.at[s, 0], beside, partner)

    def start_each(pairs):
        for condition, copy in pairs:
            pl.when(condition)(copy.start)

    def end_each(pairs):
        for condition, copy in pairs:
            pl.when(condition)(copy.wait_send)

    for s in range(layers):
        mine = layers * d + s
        halo_copy[1][s].wait_recv()
        halo_copy[0][s].wait_recv()
        tall = jnp.concatenate([halo_in[0, s], own_cut[s], halo_in[1, s]], axis=0)
        V[mine] = select_left(row_pick, tall)

        @pl.when(active)
        def _():
            copies = own_sends(s)
            if s == 0:
                start_each(copies[:2])
                pl.when(copies[2][0] & (y != 2))(copies[2][1].start)
            else:
                start_each(copies)

                @pl.when(y == 2)
                def _():
                    copies[0][1].wait_send()
                    own_sends(0)[2][1].start()

        @pl.when(jnp.logical_not(active))
        def _():
            other_send(s).start()

    per = 2 * layers

    def passing():
        low, high = (partner + depths - 2) % depths, (partner + 2) % depths

        always = y >= 0

        def home(k, slice_at, condition):
            return condition, into_window(held.at[k], slice_at, held_s.at[k, 0], beside, d)

        def window(k, slice_at, condition, where):
            return condition, into_window(held.at[k], slice_at, held_s.at[k, 1], beside, where)

        def direct(k, slice_at, condition, where):
            return condition, into_window(held.at[k], slice_at, held_s.at[k, 2], beside, where)

        def onward(k, to, condition, where):
            return condition, into_held(held.at[k], to, held_s.at[k, 2], g, where)

        first, second = layers * partner, layers * partner + 1
        to_up, to_down = needs(y + 1, y - 1), needs(y - 1, y + 1)
        here_low, here_high = needs(y, y - 1), needs(y, y + 1)
        own_low, own_high = layers * down, layers * up + 1
        part_low, part_high = layers * low, layers * high + 1
        return (
            (0, always, (
                onward(0, 3, needs(y + 2, y), up), direct(0, first, needs(y + 1, y) & ~needs(y + 2, y), up),
                window(0, first, needs(y - 1, y), down), home(0, first, always))),
            (1, always, (
                onward(1, 5, needs(y - 2, y), down), direct(1, second, needs(y - 1, y) & ~needs(y - 2, y), down),
                window(1, second, needs(y + 1, y), up), home(1, second, always))),
            (2, to_up, (window(2, own_low, to_up, up), home(2, own_low, to_up & here_low))),
            (4, to_down, (window(4, own_high, to_down, down), home(4, own_high, to_down & here_high))),
            (3, to_up, (window(3, part_low, to_up, up), home(3, part_low, to_up & here_low))),
            (5, to_down, (window(5, part_high, to_down, down), home(5, part_high, to_down & here_high))),
        )

    @pl.when(jnp.logical_not(active))
    def _():
        for k, comes, copies in passing():
            @pl.when(comes)
            def _():
                into_held(held.at[k], k, held_s.at[k, 0], beside, d).wait_recv()
                if k == 0:
                    pl.when(copies[2][0] & (y != 2))(copies[2][1].start)
                    pl.when(copies[0][0] & (y != 3))(copies[0][1].start)
                    start_each(copies[1:2] + copies[3:])
                elif k == 1:
                    pl.when(copies[2][0] & (y != 3))(copies[2][1].start)
                    start_each(copies[:2] + copies[3:])
                else:
                    start_each(copies)

                if k == 3:
                    @pl.when(y == 3)
                    def _():
                        passing()[0][2][0][1].start()
                        passing()[1][2][2][1].start()

            if k == 1:
                @pl.when(y == 2)
                def _():
                    copies[0][1].wait_send()
                    passing()[0][2][2][1].start()

    def edge_copy(n, slot):
        return remote(
            dep_out.at[n, slot], dep_in.at[1 - n, slot % layers], dep_ss.at[n, slot],
            dep_rs.at[1 - n, slot % layers], there((before, after)[n], 2 * y + slot // layers),
        )

    def middle_copy(slot):
        return remote(dep_mid.at[slot], dep_mid.at[slot], mid_s.at[slot % layers], mid_r.at[slot % layers], there(g, partner))

    def trans(s, ar, ai):
        c, n = cs[s, 0], cs[s, 1]
        return c * ar - n * ai, c * ai + n * ar

    @pl.when(active)
    def _():
        def arrive(s):
            @pl.when(s // layers != d)
            def _():
                into_window(V.at[s], s, send_v.at[0, 0], g, partner).wait_recv()

        def prepare(s):
            arrive(s)
            c, n = sincos(V[s])
            cs[s, 0] = c
            cs[s, 1] = n

        ready = jnp.where(y == 0, layers * core, per * y)
        ready_end = jnp.where(y == 0, 2 * layers * core, jnp.where(y == 2, slices, per * (y + 1)))

        def wave_copy(k, to, where):
            return remote(wave_out.at[k], wave_in.at[to], wave_s.at[k], wave_r.at[to], there(g, where))

        @pl.loop(ready, ready_end)
        def _(s):
            prepare(s)

        @pl.when(y >= 2)
        def _():
            for c in (0, 1):
                wave_copy(c, c, down).wait_recv()
                ps[c] = wave_in[c]

        def enter(s):
            @pl.when((s < ready) | (s >= ready_end))
            def _():
                prepare(s)

            c, n = cs[s, 0], cs[s, 1]
            ar, ai = ps[0], ps[1]
            ur, ui = c * ar - n * ai, c * ai + n * ar

            @pl.when(s // per == y)
            def _():
                us[s % per, 0] = ur
                us[s % per, 1] = ui

            return ur, ui

        def leave(s, qr, qi):
            @pl.when(s // per == y)
            def _():
                slot = s % per
                tall = select_left(row_back, -0.5 * (qr * us[slot, 1] + qi * us[slot, 0]))
                dep_out[0, slot] = tall[:strip]
                edge_copy(0, slot).start()
                dep_out[1, slot] = tall[2 * strip :]
                edge_copy(1, slot).start()
                dep_mid[slot] = tall[strip : 2 * strip]

                @pl.when(slot // layers != xl)
                def _():
                    middle_copy(slot).start()

        @pl.loop(jnp.where(y < 2, 0, per * y), slices - 1)
        def _(s):
            ur, ui = enter(s)
            ps[0], ps[1] = propagate(ur, ui, T)

            @pl.when((y == 1) & (s == 2 * per - 1))
            def _():
                wave_out[0] = ps[0]
                wave_copy(0, 0, up).start()

            @pl.when((y == 0) & (s == 2 * per - 1))
            def _():
                wave_out[0] = ps[1]
                wave_copy(0, 1, across).start()

            @pl.when((y == 0) & (s == 3 * per - 1))
            def _():
                for c in (0, 1):
                    wave_out[1 + c] = ps[c]
                    wave_copy(1 + c, c, down).start()

        ur, ui = enter(slices - 1)
        qr, qi = detector(ur, ui, i_ref[0], Fr, phase)

        @pl.when(y < 2)
        def _():
            wave_copy(0, 0, up).wait_send()

        @pl.when(y == 0)
        def _():
            for c in (0, 1):
                wave_copy(1 + c, c, down).wait_send()

        ps[0] = qr
        ps[1] = qi
        leave(slices - 1, qr, qi)

        @pl.loop(0, slices - 1 - per * y)
        def _(t):
            s = slices - 2 - t
            gr, gi = trans(s + 1, ps[0], ps[1])
            qr, qi = propagate(gr, gi, T)
            ps[0] = qr
            ps[1] = qi
            leave(s, qr, qi)

    for s in (1, 0):
        slot = layers * xl + s

        @pl.when(jnp.logical_not(active))
        def _():
            middle_copy(slot).wait_recv()

        total = spread(dep_mid[slot], pick[2])
        for n in near_first:
            remote(dep_out.at[n, slot], dep_in.at[n, s], dep_ss.at[n, slot], dep_rs.at[n, s], near[0]).wait_recv()
            total += spread(dep_in[n, s], pick[n])
        o_ref[s] = total

    for n in (0, 1):
        pos_copy[n].wait_send()
        for s in range(layers):
            halo_copy[n][s].wait_send()

    @pl.when(jnp.logical_not(active))
    def _():
        for s in range(layers):
            other_send(s).wait_send()
        for k, comes, copies in passing():
            if k == 1:
                end_each(copies[1:])
                pl.when(copies[0][0] & (y != 2))(copies[0][1].wait_send)
            else:
                end_each(copies)

    @pl.when(active)
    def _():
        for s in range(layers):
            copies = own_sends(s)
            if s == 0:
                end_each(copies)
            else:
                end_each(copies[1:])
                pl.when(copies[0][0] & (y != 2))(copies[0][1].wait_send)
            middle_copy(layers * (1 - xl) + s).wait_send()
        for slot in range(per):
            for n in (0, 1):
                edge_copy(n, slot).wait_send()


def local(potential, probe, positions, intensity):
    layers, strip, columns = potential.shape
    groups = lax.axis_size("probe")
    depths = lax.axis_size("depth")
    slices = layers * depths
    T, Fr, phase = tables()
    vm = pl.BlockSpec(memory_space=pltpu.VMEM)
    far = pl.BlockSpec(memory_space=pl.ANY)
    dma = pltpu.SemaphoreType.DMA
    return pl.pallas_call(
        functools.partial(kernel, groups, depths),
        out_shape=jax.ShapeDtypeStruct(potential.shape, f32),
        in_specs=[far, far, pl.BlockSpec(memory_space=pltpu.SMEM), far, far, far, far],
        out_specs=vm,
        scratch_shapes=[
            pltpu.VMEM((slices, W, W), f32),
            pltpu.VMEM((6, W, W), f32),
            pltpu.VMEM((2, W, W), f32),
            pltpu.VMEM((3, W, W), f32),
            pltpu.VMEM((slices, 2, W, W), f32),
            pltpu.VMEM((2 * layers, 2, W, W), f32),
            pltpu.VMEM((2, W, W), f32),
            pltpu.VMEM((2, 8, 128), jnp.int32),
            pltpu.VMEM((2, 2, 8, 128), jnp.int32),
            pltpu.VMEM((2, layers, strip, W), f32),
            pltpu.VMEM((2, layers, strip, W), f32),
            pltpu.VMEM((2, 2 * layers, strip, W), f32),
            pltpu.VMEM((2 * layers, strip, W), f32),
            pltpu.VMEM((2, layers, strip, W), f32),
            pltpu.VMEM((layers, strip, W), f32),
            pltpu.VMEM((3, columns, W), bf16),
            dma((2,)), dma((2,)), dma((2, layers)), dma((2, layers)),
            dma((layers, 2)), dma((slices,)), dma((6, 3)), dma((6,)),
            dma((2, 2 * layers)), dma((2, layers)), dma((layers,)), dma((layers,)),
            dma((3,)), dma((2,)),
            pltpu.VMEM(potential.shape, f32),
            pltpu.VMEM(probe.shape, f32),
            pltpu.VMEM(intensity.shape, f32),
            pltpu.VMEM(T.shape, bf16),
            pltpu.VMEM(Fr.shape, bf16),
            pltpu.VMEM(phase.shape, f32),
            dma((6,)),
        ],
        compiler_params=pltpu.CompilerParams(
            collective_id=0, has_side_effects=True, vmem_limit_bytes=56 << 20
        ),
    )(potential, probe, positions, intensity, jnp.asarray(T), jnp.asarray(Fr), jnp.asarray(phase))


def solution(mesh):
    in_specs = (P("depth", "probe", None), P(), P("probe", None), P("probe", None, None))
    out_specs = P("depth", "probe", None)
    return jax.shard_map(local, mesh=mesh, in_specs=in_specs, out_specs=out_specs, check_vma=False)
```
